32 devices in a mesh: member: 2 (over x), shard: 16 (over z, y, core).
Axes of the slice: x: 2, y: 2, z: 4, core: 2. Of those that a mesh axis runs over, the one named last changes fastest.
Arguments:
- tokens: bfloat16 [1024, 4096], P(('member', 'shard')), may hold values from -6 to 6
- key_weight: bfloat16 [4096, 16384], P(None, 'shard'), may hold values from -0.09375 to 0.09375
- value_weight: bfloat16 [16384, 4096], P('shard'), may hold values from -0.046875 to 0.046875
- shift_mix: bfloat16 [4096], replicated, may hold values from 0.049804688 to 0.94921875
- key_left: bfloat16 [16, 4096], P('member'), may hold values from -6 to 6
- key_right: bfloat16 [16, 16384], P('member', 'shard'), may hold values from -6 to 6
- value_left: bfloat16 [16, 16384], P('member', 'shard'), may hold values from -6 to 6
- value_right: bfloat16 [16, 4096], P('member'), may hold values from -6 to 6
- ranks: int32 [16], P('member'), may hold values from 0 to 15, each once
Outputs:
- mixed_out: bfloat16 [1024, 4096], P(('member', 'shard'))
- key_update: float32 [4096, 16384], P('member', 'shard')
- value_update: float32 [16384, 4096], P('shard', 'member')
The draws below stay inside these ranges and needn't reach their ends.
Inputs may be any that keep to these rules, and one draw needn't show every extreme that they name: `ranks`: each value of 0 to 15 appears exactly once.
All inputs are finite; a program needn't handle non-finite values.
Results may differ from the reference program's by a relative error of at most 0.006.
Values may be sent and summed in bfloat16 or wider, within the bound.
No kernel may reach another device: no remote copies, remote signals or barrier semaphores. Data moves between devices by JAX's collectives and lax.ppermute only.
A program may use at most 128 MiB of HBM per device.

```python
import math
import jax
import jax.numpy as jnp
from jax import lax

D = 4096
FF = 16384
LEN = 64
MEMBERS = 16
TOKENS = 1024


def block_scale(own_key, shape, cuts, least, top_value):
    level, own = 1.0, jax.random.fold_in(own_key, 6)
    for dim, shards_of in cuts:
        draws = jnp.exp(jax.random.uniform(jax.random.fold_in(own, dim), (shards_of,), jnp.float32, least / len(cuts), top_value / len(cuts)))
        level = level * jnp.repeat(draws, shape[dim] // shards_of).reshape([-1 if axis == dim else 1 for axis in range(len(shape))])
    return level


def noise(own_key, extent, spread, most, shards=(), kind=jnp.bfloat16):
    array = spread * jax.random.normal(own_key, extent, jnp.float32)
    if shards:
        array = array * block_scale(own_key, extent, shards, -0.22, 0.18)
    return jnp.clip(array, -most, most).astype(kind)


def setup_inputs(seed: int = 0) -> dict:
    arg_keys = jax.random.split(jax.random.key(seed), 10)
    return {
        "tokens": noise(arg_keys[0], (TOKENS, D), 1.0, 6.0, ((0, 32),)),
        "key_weight": noise(arg_keys[1], (D, FF), D ** -0.5, 0.09375, ((1, 16),)),
        "value_weight": noise(arg_keys[2], (FF, D), FF ** -0.5, 0.046875, ((0, 16),)),
        "shift_mix": jnp.clip(jax.random.uniform(arg_keys[3], (D,), jnp.float32, 0.049804688, 0.94921875), 0.049804688, 0.94921875).astype(jnp.bfloat16),
        "key_left": noise(arg_keys[4], (MEMBERS, D), 1.0, 6.0, ((0, 2),)),
        "key_right": noise(arg_keys[5], (MEMBERS, FF), 1.0, 6.0, ((0, 2), (1, 16))),
        "value_left": noise(arg_keys[6], (MEMBERS, FF), 1.0, 6.0, ((0, 2), (1, 16))),
        "value_right": noise(arg_keys[7], (MEMBERS, D), 1.0, 6.0, ((0, 2),)),
        "ranks": jax.random.permutation(arg_keys[8], MEMBERS).astype(jnp.int32),
    }


def reference(tokens, key_weight, value_weight, shift_mix, key_left, key_right, value_left, value_right, ranks):
    total = tokens.shape[0]
    place = jnp.arange(total, dtype=jnp.int32)
    owner = place // LEN
    previous = jnp.concatenate([jnp.zeros((1, tokens.shape[1]), tokens.dtype), tokens[:-1]], 0)
    previous = jnp.where((place % LEN == 0)[:, None], jnp.zeros_like(previous), previous)
    current = tokens.astype(jnp.float32)
    shifted = (current + (previous.astype(jnp.float32) - current) * shift_mix.astype(jnp.float32)).astype(jnp.bfloat16)
    along_all = jnp.dot(shifted, key_left.T, preferred_element_type=jnp.float32)
    along = jnp.take_along_axis(along_all, owner[:, None], 1)[:, 0]
    hidden = jnp.dot(shifted, key_weight, preferred_element_type=jnp.float32)
    hidden = hidden + 0.5 / math.sqrt(D) * along[:, None] * key_right[owner].astype(jnp.float32)
    keyed = jnp.square(jnp.maximum(hidden, 0.0)).astype(jnp.bfloat16)
    across_all = jnp.dot(keyed, value_left.T, preferred_element_type=jnp.float32)
    across = jnp.take_along_axis(across_all, owner[:, None], 1)[:, 0]
    result = jnp.dot(keyed, value_weight, preferred_element_type=jnp.float32)
    result = result + 0.5 / math.sqrt(FF) * across[:, None] * value_right[owner].astype(jnp.float32)
    mixed_out = result.astype(jnp.bfloat16)
    fitness = ranks.astype(jnp.float32) / (MEMBERS - 1) - 0.5
    factor = 2.0 / math.sqrt(MEMBERS)
    weighted_left = fitness[:, None] * key_left.astype(jnp.float32)
    key_update = jnp.dot(weighted_left.T, key_right.astype(jnp.float32), precision=lax.Precision.HIGHEST) * factor
    weighted_right = fitness[:, None] * value_right.astype(jnp.float32)
    value_update = jnp.dot(value_left.astype(jnp.float32).T, weighted_right, precision=lax.Precision.HIGHEST) * factor
    return (mixed_out, key_update, value_update)
```

```python
import functools
import math

import jax
import jax.numpy as jnp
from jax import lax
from jax.experimental import pallas as pl
from jax.experimental.pallas import tpu as pltpu
from jax.sharding import PartitionSpec as P

D = 4096
FF = 16384
LEN = 64
PLANES = 4
CORES = 2


def chunk_kernel(rows, columns, where, *refs):
    own, other = refs[:columns], refs[columns : 2 * columns]
    mix, key_left, key_right, value_left, value_right, key, value = refs[2 * columns : 2 * columns + 7]
    keep, send, whole, total, dots, natural, relative, across = refs[2 * columns + 7 :]
    step = pl.program_id(0)
    plane, y, core = where[0], where[1], where[2]
    depth, width = key.shape[0], value.shape[1]
    first = D // depth
    tokens = rows * columns * CORES

    def place(j, c):
        return pl.multiple_of(((y ^ j) * CORES + c) * rows, rows)

    def pick(array, member):
        at = lax.broadcasted_iota(jnp.int32, array.shape, 0) == member
        return jnp.sum(jnp.where(at, array.astype(jnp.float32), 0.0), 0, keepdims=True)

    def by_member(value_of):
        return [
            value_of(slice(m * LEN, (m + 1) * LEN), plane * (tokens // LEN) + m)
            for m in range(tokens // LEN)
        ]

    @pl.when(step == 0)
    def _():
        for j in range(columns):
            whole[pl.ds(place(j, core), rows), :] = own[j][...]
            whole[pl.ds(place(j, 1 - core), rows), :] = other[j][...]
        total[...] = jnp.zeros_like(total)
        dots[...] = jnp.zeros_like(dots)

    @pl.when(step < first)
    def _():
        at = pl.ds(pl.multiple_of(step * depth, depth), depth)
        current = whole[:, at].astype(jnp.float32)
        inside = lax.broadcasted_iota(jnp.int32, (tokens, 1), 0) % LEN != 0
        previous = jnp.where(inside, pltpu.roll(current, 1, 0), 0.0)
        shifted = (current + (previous - current) * mix[:, at].astype(jnp.float32)).astype(jnp.bfloat16)
        wide = shifted.astype(jnp.float32)
        left = key_left[:, at]
        products = jnp.concatenate(by_member(lambda at_rows, m: wide[at_rows] * pick(left, m)), 0)
        dots[...] += sum(products[:, i : i + 128] for i in range(0, depth, 128))
        total[...] += jnp.dot(shifted, key[...], preferred_element_type=jnp.float32)

    @pl.when(step == first - 1)
    def _():
        along = 0.5 / math.sqrt(D) * jnp.sum(dots[...], 1, keepdims=True)

        def finish(at_rows, m):
            hidden = total[at_rows, :] + along[at_rows] * pick(key_right[...], m)
            keyed = jnp.square(jnp.maximum(hidden, 0.0)).astype(jnp.bfloat16)
            natural[at_rows, :] = keyed
            sums = jnp.sum(keyed.astype(jnp.float32) * pick(value_left[...], m), 1, keepdims=True)
            dots[at_rows, :] = jnp.broadcast_to(0.5 / math.sqrt(FF) * sums, (LEN, 128))

        by_member(finish)
        for c in range(CORES):
            for j in range(columns):
                to = pl.ds((c * columns + j) * rows, rows)
                at_rows = pl.ds(place(j, core if c == 0 else 1 - core), rows)
                relative[to, :] = natural[at_rows, :]
                across[to, :] = dots[at_rows, :]

    @pl.when(step >= first)
    def _():
        result = jnp.dot(relative[...], value[...], preferred_element_type=jnp.float32)
        for c, out in enumerate((keep, send)):
            for j in range(columns):
                to = slice((c * columns + j) * rows, (c * columns + j + 1) * rows)
                m = plane * (tokens // LEN) + place(j, core if c == 0 else 1 - core) // LEN
                term = across[to, :1] * pick(value_right[...], m)
                out[j * rows : (j + 1) * rows, :] = (result[to] + term).astype(jnp.bfloat16)


def chunk(where, own, other, mix, key_left, key_right, value_left, value_right, key, value):
    columns, rows = len(own), own[0].shape[0]
    hidden = key.shape[1]
    memb = key_left.shape[0]
    depth = width = 1024
    first, second = D // depth, D // width
    tokens = rows * columns * CORES
    half = columns * rows

    def whole(shape):
        return pl.BlockSpec(shape, lambda i, _: (0, 0))

    return pl.pallas_call(
        functools.partial(chunk_kernel, rows, columns),
        out_shape=[jax.ShapeDtypeStruct((half, D), jnp.bfloat16)] * 2,
        grid_spec=pltpu.PrefetchScalarGridSpec(
            num_scalar_prefetch=1,
            grid=(first + second,),
            in_specs=[whole((rows, D))] * (2 * columns)
            + [whole((1, D)), whole((memb, D)), whole((memb, hidden)), whole((memb, hidden))]
            + [
                pl.BlockSpec((memb, width), lambda i, _: (0, jnp.maximum(i - first, 0))),
                pl.BlockSpec((depth, hidden), lambda i, _: (jnp.minimum(i, first - 1), 0)),
                pl.BlockSpec((hidden, width), lambda i, _: (0, jnp.maximum(i - first, 0))),
            ],
            out_specs=[pl.BlockSpec((half, width), lambda i, _: (0, jnp.maximum(i - first, 0)))] * 2,
            scratch_shapes=[
                pltpu.VMEM((tokens, D), jnp.bfloat16),
                pltpu.VMEM((tokens, hidden), jnp.float32),
                pltpu.VMEM((tokens, 128), jnp.float32),
                pltpu.VMEM((tokens, hidden), jnp.bfloat16),
                pltpu.VMEM((tokens, hidden), jnp.bfloat16),
                pltpu.VMEM((tokens, 128), jnp.float32),
            ],
        ),
        compiler_params=pltpu.CompilerParams(vmem_limit_bytes=32 * 1024 * 1024),
        cost_estimate=pl.CostEstimate(
            flops=4 * tokens * D * hidden, bytes_accessed=4 * D * hidden, transcendentals=0
        ),
    )(where, *own, *other, mix, key_left, key_right, value_left, value_right, key, value)


def updates(key_left, key_right, value_left, value_right, ranks):
    memb, hidden = key_right.shape
    marks = jnp.broadcast_to(ranks.astype(jnp.bfloat16)[:, None], (memb, 128))
    pack = jnp.concatenate([key_left, value_right, key_right, value_left, marks], 1)
    pack = lax.all_gather(pack, "member", axis=0, tiled=True)
    everyone = pack.shape[0]
    part = D // lax.axis_size("member")
    start = lax.axis_index("member") * part
    left = lax.dynamic_slice_in_dim(pack, start, part, 1)
    right = lax.dynamic_slice_in_dim(pack, D + start, part, 1)
    key_side, value_side = pack[:, 2 * D : 2 * D + hidden], pack[:, 2 * D + hidden : 2 * D + 2 * hidden]
    fitness = pack[:, -1:].astype(jnp.float32) / (everyone - 1) - 0.5
    weight = 2.0 / math.sqrt(everyone) * fitness

    def split(array):
        rest, terms = weight * array.astype(jnp.float32), []
        for _ in range(3):
            terms.append(lax.reduce_precision(rest, 8, 7).astype(jnp.bfloat16))
            rest = rest - terms[-1].astype(jnp.float32)
        return jnp.concatenate(terms, 0)

    def thrice(array):
        return jnp.concatenate([array] * 3, 0)

    def outer(a, b):
        return lax.dot_general(a, b, (((0,), (0,)), ((), ())), preferred_element_type=jnp.float32)

    return outer(split(left), thrice(key_side)), outer(thrice(value_side), split(right))


def local(
    tokens, key_weight, value_weight, shift_mix, key_left, key_right, value_left, value_right, ranks
):
    devices = lax.axis_size("shard")
    columns = devices // (PLANES * CORES)
    rows = tokens.shape[0]
    me = lax.axis_index("shard")
    z, y, core = me // (columns * CORES), me // CORES % columns, me % CORES

    def swap(array, bits):
        return lax.ppermute(array, "shard", [(i, i ^ bits) for i in range(devices)])

    key_update, value_update = updates(key_left, key_right, value_left, value_right, ranks)

    def plane_bits(k):
        return k * columns * CORES

    mix = shift_mix[None, :]
    arrived = [tokens] + [swap(tokens, plane_bits(k)) for k in range(1, PLANES)]
    partial = []
    for k in range(PLANES):
        own = [arrived[k]] + [swap(arrived[k], j * CORES) for j in range(1, columns)]
        other = [swap(block, 1) for block in own]
        where = jnp.stack([z ^ k, y, core]).astype(jnp.int32)
        partial.append(
            chunk(
                where, own, other, mix, key_left, key_right, value_left, value_right, key_weight, value_weight
            )
        )
    result = 0.0
    for k in reversed(range(PLANES)):
        keep, send = partial[k]
        both = keep.astype(jnp.float32) + swap(send, 1).astype(jnp.float32)
        mine = both[:rows]
        for j in range(1, columns):
            term = both[j * rows : (j + 1) * rows].astype(jnp.bfloat16)
            mine = mine + swap(term, j * CORES).astype(jnp.float32)
        if k:
            mine = swap(mine.astype(jnp.bfloat16), plane_bits(k)).astype(jnp.float32)
        result = result + mine
    return result.astype(jnp.bfloat16), key_update, value_update


def solution(mesh):
    placed = (
        P(("member", "shard"), None),
        P(None, "shard"),
        P("shard", None),
        P(),
        P("member", None),
        P("member", "shard"),
        P("member", "shard"),
        P("member", None),
        P("member"),
    )
    return jax.shard_map(
        local,
        mesh=mesh,
        in_specs=placed,
        out_specs=(P(("member", "shard"), None), P("member", "shard"), P("shard", "member")),
        check_vma=False,
    )
```

```python
import functools
import math

import jax
import jax.numpy as jnp
from jax import lax
from jax.experimental import pallas as pl
from jax.experimental.pallas import tpu as pltpu
from jax.sharding import PartitionSpec as P

D = 4096
FF = 16384
LEN = 64
PLANES = 4
CORES = 2
STEP = 1024


def chunk_kernel(rows, columns, where, *refs):
    own, other = refs[:columns], refs[columns : 2 * columns]
    mix, key_left, key_right, value_left, value_right, key, value = refs[2 * columns : 2 * columns + 7]
    keep, send, whole, natural, relative, natural_dots, dots = refs[2 * columns + 7 :]
    plane, y, core = where[0], where[1], where[2]
    tokens = rows * columns * CORES
    members = tokens // LEN

    def place(j, c):
        return pl.multiple_of(((y ^ j) * CORES + c) * rows, rows)

    def pick(array, member):
        at = lax.broadcasted_iota(jnp.int32, array.shape, 0) == member
        return jnp.sum(jnp.where(at, array.astype(jnp.float32), 0.0), 0, keepdims=True)

    for j in range(columns):
        whole[pl.ds(place(j, core), rows), :] = own[j][...]
        whole[pl.ds(place(j, 1 - core), rows), :] = other[j][...]

    inside = lax.broadcasted_iota(jnp.int32, (tokens, 1), 0) % LEN != 0
    total, along = None, [0.0] * members
    for start in range(0, D, STEP):
        at = slice(start, start + STEP)
        current = whole[:, at].astype(jnp.float32)
        previous = jnp.where(inside, pltpu.roll(current, 1, 0), 0.0)
        shifted = (current + (previous - current) * mix[:, at].astype(jnp.float32)).astype(jnp.bfloat16)
        part = jnp.dot(shifted, key[at, :], preferred_element_type=jnp.float32)
        total = part if total is None else total + part
        for m in range(members):
            wide = shifted[m * LEN : (m + 1) * LEN].astype(jnp.float32)
            products = wide * pick(key_left[:, at], plane * members + m)
            along[m] = along[m] + sum(products[:, i : i + 128] for i in range(0, STEP, 128))

    for m in range(members):
        at = slice(m * LEN, (m + 1) * LEN)
        dot = 0.5 / math.sqrt(D) * jnp.sum(along[m], 1, keepdims=True)
        hidden = total[at] + dot * pick(key_right[...], plane * members + m)
        keyed = jnp.square(jnp.maximum(hidden, 0.0)).astype(jnp.bfloat16)
        natural[at, :] = keyed
        dot = jnp.sum(keyed.astype(jnp.float32) * pick(value_left[...], plane * members + m), 1, keepdims=True)
        natural_dots[at, :] = jnp.broadcast_to(0.5 / math.sqrt(FF) * dot, (LEN, 128))

    cores = (core, 1 - core)
    for c in range(CORES):
        for j in range(columns):
            to = slice((c * columns + j) * rows, (c * columns + j + 1) * rows)
            relative[to, :] = natural[pl.ds(place(j, cores[c]), rows), :]
            dots[to, :] = natural_dots[pl.ds(place(j, cores[c]), rows), :]

    for start in range(0, D, STEP):
        at = slice(start, start + STEP)
        result = jnp.dot(relative[...], value[:, at], preferred_element_type=jnp.float32)
        for c, out in enumerate((keep, send)):
            for j in range(columns):
                to = slice((c * columns + j) * rows, (c * columns + j + 1) * rows)
                right = pick(value_right[:, at], plane * members + place(j, cores[c]) // LEN)
                out[j * rows : (j + 1) * rows, at] = (result[to] + dots[to, :1] * right).astype(jnp.bfloat16)


def chunk(where, own, other, mix, key_left, key_right, value_left, value_right, key, value):
    columns, rows = len(own), own[0].shape[0]
    hidden = key.shape[1]
    tokens = rows * columns * CORES
    operands = (*own, *other, mix, key_left, key_right, value_left, value_right, key, value)
    return pl.pallas_call(
        functools.partial(chunk_kernel, rows, columns),
        out_shape=[jax.ShapeDtypeStruct((columns * rows, D), jnp.bfloat16)] * 2,
        in_specs=[pl.BlockSpec(memory_space=pltpu.SMEM)]
        + [pl.BlockSpec(memory_space=pltpu.VMEM)] * len(operands),
        out_specs=[pl.BlockSpec(memory_space=pltpu.VMEM)] * 2,
        scratch_shapes=[
            pltpu.VMEM((tokens, D), jnp.bfloat16),
            pltpu.VMEM((tokens, hidden), jnp.bfloat16),
            pltpu.VMEM((tokens, hidden), jnp.bfloat16),
            pltpu.VMEM((tokens, 128), jnp.float32),
            pltpu.VMEM((tokens, 128), jnp.float32),
        ],
        compiler_params=pltpu.CompilerParams(vmem_limit_bytes=28 * 1024 * 1024),
        cost_estimate=pl.CostEstimate(
            flops=4 * tokens * D * hidden, bytes_accessed=4 * D * hidden, transcendentals=0
        ),
    )(where, *operands)


def pack_members(key_left, key_right, value_left, value_right, ranks):
    marks = jnp.broadcast_to(ranks.astype(jnp.bfloat16)[:, None], (ranks.shape[0], 128))
    return jnp.concatenate([key_left, value_right, key_right, value_left, marks], 1)


def member_sides(packs, hidden):
    pack = jnp.concatenate(packs, 0)
    everyone = pack.shape[0]
    part = D // lax.axis_size("member")
    start = lax.axis_index("member") * part
    left = lax.dynamic_slice_in_dim(pack, start, part, 1)
    right = lax.dynamic_slice_in_dim(pack, D + start, part, 1)
    key_side, value_side = pack[:, 2 * D : 2 * D + hidden], pack[:, 2 * D + hidden : 2 * D + 2 * hidden]
    fitness = pack[:, -1:].astype(jnp.float32) / (everyone - 1) - 0.5
    weight = 2.0 / math.sqrt(everyone) * fitness

    def split(array):
        rest, terms = weight * array.astype(jnp.float32), []
        for _ in range(3):
            terms.append(lax.reduce_precision(rest, 8, 7).astype(jnp.bfloat16))
            rest = rest - terms[-1].astype(jnp.float32)
        return jnp.concatenate(terms, 0)

    def thrice(array):
        return jnp.concatenate([array] * 3, 0)

    return (split(left), thrice(key_side)), (thrice(value_side), split(right))


def outer(sides):
    return lax.dot_general(*sides, (((0,), (0,)), ((), ())), preferred_element_type=jnp.float32)


def after(array, *others):
    return lax.optimization_barrier((array, *others))[0]


def local(
    tokens, key_weight, value_weight, shift_mix, key_left, key_right, value_left, value_right, ranks
):
    devices, groups = lax.axis_size("shard"), lax.axis_size("member")
    columns = devices // (PLANES * CORES)
    rows, hidden = tokens.shape[0], key_weight.shape[1]
    me = lax.axis_index("shard")
    z, y, core = me // (columns * CORES), me // CORES % columns, me % CORES
    mix = shift_mix[None, :]

    def swap(array, bits):
        return lax.ppermute(array, "shard", [(i, i ^ bits) for i in range(devices)])

    def over_z(array, k):
        return swap(array, k * columns * CORES)

    def over_y(array, j):
        return swap(array, j * CORES)

    def over_cores(array):
        return swap(array, 1)

    def partial(k, own, other):
        where = jnp.stack([z ^ k, y, core]).astype(jnp.int32)
        return chunk(
            where, own, other, mix, key_left, key_right, value_left, value_right, key_weight, value_weight
        )

    def spread(block):
        own = [block] + [over_y(block, j) for j in range(1, columns)]
        return own, [over_cores(part) for part in own]

    pack = pack_members(key_left, key_right, value_left, value_right, ranks)
    packs = [pack] + [
        lax.ppermute(pack, "member", [(i, i ^ bits) for i in range(groups)]) for bits in range(1, groups)
    ]
    key_sides, value_sides = member_sides(packs, hidden)

    arrived = [tokens, over_z(tokens, 1), over_z(tokens, 2), None]
    own0, other0 = spread(tokens)
    own1, other1 = spread(arrived[1])
    own0[0] = after(own0[0], arrived[1])
    keep0, send0 = partial(0, own0, other0)

    arrived[2] = after(arrived[2], keep0)
    arrived[3] = over_z(arrived[2], 1)
    own2, other2 = spread(arrived[2])
    key_update = outer((after(key_sides[0], keep0, arrived[2]), key_sides[1]))
    own1[0] = after(own1[0], key_update)
    keep1, send1 = partial(1, own1, other1)

    arrived[3] = after(arrived[3], keep1)
    own3, other3 = spread(arrived[3])
    own2[0] = after(own2[0], arrived[3], keep1)
    keep2, send2 = partial(2, own2, other2)

    def both_cores(keep, send):
        both = keep.astype(jnp.float32) + over_cores(send).astype(jnp.float32)
        return both[:rows], [
            both[j * rows : (j + 1) * rows].astype(jnp.bfloat16) for j in range(1, columns)
        ]

    def both_columns(mine, terms):
        for j, term in enumerate(terms, 1):
            mine = mine + over_y(term, j).astype(jnp.float32)
        return mine

    mine2, terms2 = both_cores(keep2, send2)
    own3[0] = after(own3[0], *terms2)
    keep3, send3 = partial(3, own3, other3)
    mine3, terms3 = both_cores(keep3, send3)
    send1 = after(send1, *terms3)
    send0 = after(send0, *terms3)
    value_update = outer((after(value_sides[0], *terms3), value_sides[1]))
    mine1, terms1 = both_cores(keep1, send1)
    mine0, terms0 = both_cores(keep0, send0)

    sum3 = over_z(both_columns(mine3, terms3).astype(jnp.bfloat16), 1)
    sum2 = both_columns(mine2, terms2) + sum3.astype(jnp.float32)
    sum2 = over_z(sum2.astype(jnp.bfloat16), 2)
    sum1 = over_z(both_columns(mine1, terms1).astype(jnp.bfloat16), 1)
    sum0 = both_columns(mine0, terms0)
    result = sum0 + sum1.astype(jnp.float32) + sum2.astype(jnp.float32)
    return result.astype(jnp.bfloat16), key_update, value_update


def solution(mesh):
    placed = (
        P(("member", "shard"), None),
        P(None, "shard"),
        P("shard", None),
        P(),
        P("member", None),
        P("member", "shard"),
        P("member", "shard"),
        P("member", None),
        P("member"),
    )
    return jax.shard_map(
        local,
        mesh=mesh,
        in_specs=placed,
        out_specs=(P(("member", "shard"), None), P("member", "shard"), P("shard", "member")),
        check_vma=False,
    )
```

```python
import functools
import math

import jax
import jax.numpy as jnp
from jax import lax
from jax.experimental import pallas as pl
from jax.experimental.pallas import tpu as pltpu
from jax.sharding import PartitionSpec as P

D = 4096
FF = 16384
LEN = 64
PLANES = 4
CORES = 2
STEP = 1024


def chunk_kernel(k, rows, columns, *refs):
    own, other = refs[:columns], refs[columns : 2 * columns]
    mix, key_left, key_right, value_left, value_right, key, value = refs[2 * columns : 2 * columns + 7]
    keep, send, whole, natural, relative, natural_dots, dots = refs[2 * columns + 7 :]
    me = lax.axis_index("shard")
    core, y, plane = me % CORES, me // CORES % columns, me // (CORES * columns) ^ k
    tokens = rows * columns * CORES
    members = tokens // LEN

    def place(j, c):
        return pl.multiple_of(((y ^ j) * CORES + c) * rows, rows)

    def pick(array, member):
        at = lax.broadcasted_iota(jnp.int32, array.shape, 0) == member
        return jnp.sum(jnp.where(at, array.astype(jnp.float32), 0.0), 0, keepdims=True)

    for j in range(columns):
        whole[pl.ds(place(j, core), rows), :] = own[j][...]
        whole[pl.ds(place(j, 1 - core), rows), :] = other[j][...]

    inside = lax.broadcasted_iota(jnp.int32, (tokens, 1), 0) % LEN != 0
    total, along = None, [0.0] * members
    for start in range(0, D, STEP):
        at = slice(start, start + STEP)
        current = whole[:, at].astype(jnp.float32)
        previous = jnp.where(inside, pltpu.roll(current, 1, 0), 0.0)
        shifted = (current + (previous - current) * mix[:, at].astype(jnp.float32)).astype(jnp.bfloat16)
        part = jnp.dot(shifted, key[at, :], preferred_element_type=jnp.float32)
        total = part if total is None else total + part
        for m in range(members):
            wide = shifted[m * LEN : (m + 1) * LEN].astype(jnp.float32)
            products = wide * pick(key_left[:, at], plane * members + m)
            along[m] = along[m] + sum(products[:, i : i + 128] for i in range(0, STEP, 128))

    for m in range(members):
        at = slice(m * LEN, (m + 1) * LEN)
        dot = 0.5 / math.sqrt(D) * jnp.sum(along[m], 1, keepdims=True)
        hidden = total[at] + dot * pick(key_right[...], plane * members + m)
        keyed = jnp.square(jnp.maximum(hidden, 0.0)).astype(jnp.bfloat16)
        natural[at, :] = keyed
        dot = jnp.sum(keyed.astype(jnp.float32) * pick(value_left[...], plane * members + m), 1, keepdims=True)
        natural_dots[at, :] = jnp.broadcast_to(0.5 / math.sqrt(FF) * dot, (LEN, 128))

    cores = (core, 1 - core)
    for c in range(CORES):
        for j in range(columns):
            to = slice((c * columns + j) * rows, (c * columns + j + 1) * rows)
            relative[to, :] = natural[pl.ds(place(j, cores[c]), rows), :]
            dots[to, :] = natural_dots[pl.ds(place(j, cores[c]), rows), :]

    for start in range(0, D, STEP):
        at = slice(start, start + STEP)
        result = jnp.dot(relative[...], value[:, at], preferred_element_type=jnp.float32)
        for c, out in enumerate((keep, send)):
            for j in range(columns):
                to = slice((c * columns + j) * rows, (c * columns + j + 1) * rows)
                right = pick(value_right[:, at], plane * members + place(j, cores[c]) // LEN)
                out[j * rows : (j + 1) * rows, at] = (result[to] + dots[to, :1] * right).astype(jnp.bfloat16)


def chunk(k, own, other, mix, key_left, key_right, value_left, value_right, key, value):
    columns, rows = len(own), own[0].shape[0]
    hidden = key.shape[1]
    tokens = rows * columns * CORES
    operands = (*own, *other, mix, key_left, key_right, value_left, value_right, key, value)
    return pl.pallas_call(
        functools.partial(chunk_kernel, k, rows, columns),
        out_shape=[jax.ShapeDtypeStruct((columns * rows, D), jnp.bfloat16)] * 2,
        in_specs=[pl.BlockSpec(memory_space=pltpu.VMEM)] * len(operands),
        out_specs=[pl.BlockSpec(memory_space=pltpu.VMEM)] * 2,
        scratch_shapes=[
            pltpu.VMEM((tokens, D), jnp.bfloat16),
            pltpu.VMEM((tokens, hidden), jnp.bfloat16),
            pltpu.VMEM((tokens, hidden), jnp.bfloat16),
            pltpu.VMEM((tokens, 128), jnp.float32),
            pltpu.VMEM((tokens, 128), jnp.float32),
        ],
        compiler_params=pltpu.CompilerParams(vmem_limit_bytes=8 * 1024 * 1024),
        cost_estimate=pl.CostEstimate(flops=tokens, bytes_accessed=tokens, transcendentals=0),
    )(*operands)


def sum_kernel(rows, keep, arrived, mine, *terms):
    both = keep[...].astype(jnp.float32) + arrived[...].astype(jnp.float32)
    mine[...] = both[:rows].astype(mine.dtype)
    per = D // terms[0].shape[1]
    for i, term in enumerate(terms):
        j, at = i // per + 1, i % per * term.shape[1]
        term[...] = both[j * rows : (j + 1) * rows, at : at + term.shape[1]].astype(jnp.bfloat16)


def sum_cores(keep, arrived, columns, per, kind=jnp.float32):
    rows = keep.shape[0] // columns
    terms = [jax.ShapeDtypeStruct((rows, D // per), jnp.bfloat16)] * ((columns - 1) * per)
    mine, *terms = pl.pallas_call(
        functools.partial(sum_kernel, rows),
        out_shape=[jax.ShapeDtypeStruct((rows, D), kind)] + terms,
        in_specs=[pl.BlockSpec(memory_space=pltpu.VMEM)] * 2,
        out_specs=[pl.BlockSpec(memory_space=pltpu.VMEM)] * (1 + len(terms)),
        compiler_params=pltpu.CompilerParams(vmem_limit_bytes=8 * 1024 * 1024),
        cost_estimate=pl.CostEstimate(flops=rows, bytes_accessed=rows, transcendentals=0),
    )(keep, arrived)
    return mine, [terms[i::per] for i in range(per)]


def pack_kernel(ranks, *refs):
    parts, out = refs[:-1], refs[-1]
    at = 0
    for part in parts:
        out[:, at : at + part.shape[1]] = part[...]
        at += part.shape[1]
    row = lax.broadcasted_iota(jnp.int32, (ranks.shape[0], 128), 0)
    marks = sum(jnp.where(row == m, ranks[m], 0) for m in range(ranks.shape[0]))
    out[:, at:] = marks.astype(jnp.float32).astype(jnp.bfloat16)


def pack_members(key_left, key_right, value_left, value_right, ranks):
    parts = (key_left, value_right, key_right, value_left)
    wide = sum(part.shape[1] for part in parts) + 128
    return pl.pallas_call(
        pack_kernel,
        out_shape=jax.ShapeDtypeStruct((ranks.shape[0], wide), jnp.bfloat16),
        in_specs=[pl.BlockSpec(memory_space=pltpu.SMEM)] + [pl.BlockSpec(memory_space=pltpu.VMEM)] * 4,
        out_specs=pl.BlockSpec(memory_space=pltpu.VMEM),
        compiler_params=pltpu.CompilerParams(vmem_limit_bytes=4 * 1024 * 1024),
        cost_estimate=pl.CostEstimate(flops=wide, bytes_accessed=wide, transcendentals=0),
    )(ranks, *parts)


def load_kernel(*refs):
    count = len(refs) // 2
    sems = refs[-1]
    copies = [pltpu.make_async_copy(refs[i], refs[count + i], sems.at[i]) for i in range(count)]
    for copy in copies:
        copy.start()
    for copy in copies:
        copy.wait()


def load(*arrays):
    size = sum(array.size * array.dtype.itemsize for array in arrays)
    return pl.pallas_call(
        load_kernel,
        out_shape=[jax.ShapeDtypeStruct(array.shape, array.dtype) for array in arrays],
        in_specs=[pl.BlockSpec(memory_space=pltpu.HBM)] * len(arrays),
        out_specs=[pl.BlockSpec(memory_space=pltpu.VMEM)] * len(arrays),
        scratch_shapes=[pltpu.SemaphoreType.DMA((len(arrays),))],
        compiler_params=pltpu.CompilerParams(vmem_limit_bytes=1024 * 1024),
        cost_estimate=pl.CostEstimate(flops=0, bytes_accessed=size, transcendentals=0),
    )(*arrays)


def update_kernel(fit_rows, groups, hidden, *refs):
    *packs, out, left, right = refs
    part, rows = D // groups, out.shape[0]

    def columns(start, size):
        at = pl.ds(pl.multiple_of(start, 128), size)
        return jnp.concatenate([ref[:, at].astype(jnp.float32) for ref in packs], 0)

    def split(array):
        everyone = array.shape[0]
        fitness = columns(packs[0].shape[1] - 128, 128)[:, :1] / (everyone - 1) - 0.5
        rest, terms = 2.0 / math.sqrt(everyone) * fitness * array, []
        for _ in range(3):
            terms.append(rest.astype(jnp.bfloat16).astype(jnp.float32))
            rest = rest - terms[-1]
        return jnp.concatenate(terms, 0).astype(jnp.bfloat16)

    def thrice(array):
        return jnp.concatenate([array] * 3, 0).astype(jnp.bfloat16)

    @pl.when(pl.program_id(0) == 0)
    def _():
        half = lax.axis_index("member") * part
        if fit_rows:
            left[...], right[...] = split(columns(half, part)), thrice(columns(2 * D, hidden))
        else:
            left[...], right[...] = thrice(columns(2 * D + hidden, hidden)), split(columns(D + half, part))

    at = pl.ds(pl.multiple_of(pl.program_id(0) * rows, rows), rows)
    out[...] = lax.dot_general(
        left[:, at], right[...], (((0,), (0,)), ((), ())), preferred_element_type=jnp.float32
    )


def update(fit_rows, packs, groups, hidden):
    part = D // groups
    shape, rows = ((part, hidden), 256) if fit_rows else ((hidden, part), 128)
    depth = 3 * packs[0].shape[0] * len(packs)
    return pl.pallas_call(
        functools.partial(update_kernel, fit_rows, groups, hidden),
        out_shape=jax.ShapeDtypeStruct(shape, jnp.float32),
        grid=(shape[0] // rows,),
        in_specs=[pl.BlockSpec(memory_space=pltpu.VMEM)] * len(packs),
        out_specs=pl.BlockSpec((rows, shape[1]), lambda i: (i, 0)),
        scratch_shapes=[pltpu.VMEM((depth, shape[0]), jnp.bfloat16), pltpu.VMEM((depth, shape[1]), jnp.bfloat16)],
        compiler_params=pltpu.CompilerParams(vmem_limit_bytes=12 * 1024 * 1024),
        cost_estimate=pl.CostEstimate(flops=0, bytes_accessed=8 * shape[0] * shape[1], transcendentals=0),
    )(*packs)


def together(*values):
    return lax.optimization_barrier(values)


def local(
    tokens, key_weight, value_weight, shift_mix, key_left, key_right, value_left, value_right, ranks
):
    devices, groups = lax.axis_size("shard"), lax.axis_size("member")
    columns = devices // (PLANES * CORES)
    rows, hidden = tokens.shape[0], key_weight.shape[1]
    mix = shift_mix[None, :]
    (key,) = load(key_weight)

    def swap(array, bits):
        return lax.ppermute(array, "shard", [(i, i ^ bits) for i in range(devices)])

    def over_z(array, k):
        return swap(array, k * columns * CORES)

    def over_y(array, j):
        return swap(array, j * CORES)

    def over_cores(array):
        return swap(array, 1)

    def partial(k, own, other):
        return chunk(k, own, other, mix, key_left, key_right, value_left, value_right, key, value)

    def all_y(block):
        return [over_y(block, j) for j in range(1, columns)]

    def all_cores(blocks):
        return [over_cores(block) for block in blocks]

    def exchange_y(terms):
        return [over_y(term, j) for j, term in enumerate(terms, 1)]

    def add(mine, arrived):
        return functools.reduce(lambda total, part: total + part.astype(jnp.float32), arrived, mine)

    near, far = over_z(tokens, 1), over_z(tokens, 2)
    y0, c0 = all_y(tokens), over_cores(tokens)
    mix, key, value = together(shift_mix[None, :], key_weight, value_weight)
    key, value = load(key, value)
    near, y0, c0, key, value, pack_of = together(near, y0, c0, key, value, key_left)

    y1, c1, cy0 = all_y(near), over_cores(near), all_cores(y0)
    pack = pack_members(pack_of, key_right, value_left, value_right, ranks)
    packs = [pack] + [
        lax.ppermute(pack, "member", [(i, i ^ bits) for i in range(groups)]) for bits in range(1, groups)
    ]
    far, y1, c1, cy0, packs = together(far, y1, c1, cy0, packs)

    farthest, y2, c2, cy1 = over_z(far, 1), all_y(far), over_cores(far), all_cores(y1)
    key_update = update(True, packs, groups, hidden)
    own, key_update = together(tokens, key_update)
    keep0, send0 = partial(0, [own] + y0, [c0] + cy0)
    farthest, y2, c2, cy1, keep0, send0 = together(farthest, y2, c2, cy1, keep0, send0)

    y3, c3, cy2 = all_y(farthest), over_cores(farthest), all_cores(y2)
    keep1, send1 = partial(1, [near] + y1, [c1] + cy1)
    far, keep1 = together(far, keep1)
    keep2, send2 = partial(2, [far] + y2, [c2] + cy2)
    y3, c3, keep1, send1, keep2, send2 = together(y3, c3, keep1, send1, keep2, send2)

    cy3 = all_cores(y3)
    mine2, (terms2,) = sum_cores(keep2, over_cores(send2), columns, 1)
    mine1, (terms1,) = sum_cores(keep1, over_cores(send1), columns, 1, jnp.bfloat16)
    farthest, mine2, terms2, mine1, terms1 = together(farthest, mine2, terms2, mine1, terms1)
    back2, mine1 = exchange_y(terms2), over_z(mine1, 1)
    keep3, send3 = partial(3, [farthest] + y3, [c3] + cy3)
    back2, mine1, terms1, send0, keep3, send3 = together(back2, mine1, terms1, send0, keep3, send3)

    terms1, back0 = [over_z(term, 1) for term in terms1], over_cores(send0)
    mine3, terms3 = sum_cores(keep3, over_cores(send3), columns, 2)
    back3 = exchange_y(terms3[0])
    back3, rest3, terms1, back0 = together(back3, terms3[1], terms1, back0)

    half = D // 2
    parts = (slice(0, half), slice(half, D))
    onward = over_z(add(mine3[:, parts[0]], back3).astype(jnp.bfloat16), 1)
    back3 = exchange_y(rest3)
    both = keep0.astype(jnp.float32) + back0.astype(jnp.float32)
    mine0 = add(both[:rows], [mine1])
    terms0 = [add(both[j * rows : (j + 1) * rows], [term]) for j, term in enumerate(terms1, 1)]
    sum2 = add(mine2, back2)
    onward, back3, mine0, terms0, sum2, packs = together(onward, back3, mine0, terms0, sum2, packs)

    first = over_z((sum2[:, parts[0]] + onward.astype(jnp.float32)).astype(jnp.bfloat16), 2)
    onward = over_z(add(mine3[:, parts[1]], back3).astype(jnp.bfloat16), 1)
    back0 = exchange_y([term.astype(jnp.bfloat16) for term in terms0])
    value_update = update(False, packs, groups, hidden)
    first, onward, back0, value_update = together(first, onward, back0, value_update)

    second = over_z((sum2[:, parts[1]] + onward.astype(jnp.float32)).astype(jnp.bfloat16), 2)
    result = add(mine0, back0)
    result = [add(result[:, at], [part]) for at, part in zip(parts, (first, second))]
    return jnp.concatenate(result, 1).astype(jnp.bfloat16), key_update, value_update


def solution(mesh):
    placed = (
        P(("member", "shard"), None),
        P(None, "shard"),
        P("shard", None),
        P(),
        P("member", None),
        P("member", "shard"),
        P("member", "shard"),
        P("member", None),
        P("member"),
    )
    return jax.shard_map(
        local,
        mesh=mesh,
        in_specs=placed,
        out_specs=(P(("member", "shard"), None), P("member", "shard"), P("shard", "member")),
        check_vma=False,
    )
```

```python
import functools
import math

import jax
import jax.numpy as jnp
from jax import lax
from jax.experimental import pallas as pl
from jax.experimental.pallas import tpu as pltpu
from jax.sharding import PartitionSpec as P

D = 4096
FF = 16384
LEN = 64
PLANES = 4
CORES = 2
STEP = 1024
PARTS = 2
PIECES = 4


def chunk_kernel(k, rows, columns, *refs):
    own, other = refs[:columns], refs[columns : 2 * columns]
    mix, key_left, key_right, value_left, value_right, key, value = refs[2 * columns : 2 * columns + 7]
    keep, send, whole, natural, relative, natural_dots, dots = refs[2 * columns + 7 :]
    me = lax.axis_index("shard")
    core, y, plane = me % CORES, me // CORES % columns, me // (CORES * columns) ^ k
    tokens = rows * columns * CORES
    members = tokens // LEN

    def place(j, c):
        return pl.multiple_of(((y ^ j) * CORES + c) * rows, rows)

    def pick(array, member):
        at = lax.broadcasted_iota(jnp.int32, array.shape, 0) == member
        return jnp.sum(jnp.where(at, array.astype(jnp.float32), 0.0), 0, keepdims=True)

    for j in range(columns):
        whole[pl.ds(place(j, core), rows), :] = own[j][...]
        whole[pl.ds(place(j, 1 - core), rows), :] = other[j][...]

    inside = lax.broadcasted_iota(jnp.int32, (tokens, 1), 0) % LEN != 0
    total, along = None, [0.0] * members
    for start in range(0, D, STEP):
        at = slice(start, start + STEP)
        current = whole[:, at].astype(jnp.float32)
        previous = jnp.where(inside, pltpu.roll(current, 1, 0), 0.0)
        shifted = (current + (previous - current) * mix[:, at].astype(jnp.float32)).astype(jnp.bfloat16)
        part = jnp.dot(shifted, key[at, :], preferred_element_type=jnp.float32)
        total = part if total is None else total + part
        for m in range(members):
            wide = shifted[m * LEN : (m + 1) * LEN].astype(jnp.float32)
            products = wide * pick(key_left[:, at], plane * members + m)
            along[m] = along[m] + sum(products[:, i : i + 128] for i in range(0, STEP, 128))

    for m in range(members):
        at = slice(m * LEN, (m + 1) * LEN)
        dot = 0.5 / math.sqrt(D) * jnp.sum(along[m], 1, keepdims=True)
        hidden = total[at] + dot * pick(key_right[...], plane * members + m)
        keyed = jnp.square(jnp.maximum(hidden, 0.0)).astype(jnp.bfloat16)
        natural[at, :] = keyed
        dot = jnp.sum(keyed.astype(jnp.float32) * pick(value_left[...], plane * members + m), 1, keepdims=True)
        natural_dots[at, :] = jnp.broadcast_to(0.5 / math.sqrt(FF) * dot, (LEN, 128))

    cores = (core, 1 - core)
    for c in range(CORES):
        for j in range(columns):
            to = slice((c * columns + j) * rows, (c * columns + j + 1) * rows)
            relative[to, :] = natural[pl.ds(place(j, cores[c]), rows), :]
            dots[to, :] = natural_dots[pl.ds(place(j, cores[c]), rows), :]

    for start in range(0, D, STEP):
        at = slice(start, start + STEP)
        result = jnp.dot(relative[...], value[:, at], preferred_element_type=jnp.float32)
        for c, out in enumerate((keep, send)):
            for j in range(columns):
                to = slice((c * columns + j) * rows, (c * columns + j + 1) * rows)
                right = pick(value_right[:, at], plane * members + place(j, cores[c]) // LEN)
                out[j * rows : (j + 1) * rows, at] = (result[to] + dots[to, :1] * right).astype(jnp.bfloat16)


def chunk(k, own, other, mix, key_left, key_right, value_left, value_right, key, value):
    columns, rows = len(own), own[0].shape[0]
    hidden = key.shape[1]
    tokens = rows * columns * CORES
    operands = (*own, *other, mix, key_left, key_right, value_left, value_right, key, value)
    return pl.pallas_call(
        functools.partial(chunk_kernel, k, rows, columns),
        out_shape=[jax.ShapeDtypeStruct((columns * rows, D), jnp.bfloat16)] * 2,
        in_specs=[pl.BlockSpec(memory_space=pltpu.VMEM)] * len(operands),
        out_specs=[pl.BlockSpec(memory_space=pltpu.VMEM)] * 2,
        scratch_shapes=[
            pltpu.VMEM((tokens, D), jnp.bfloat16),
            pltpu.VMEM((tokens, hidden), jnp.bfloat16),
            pltpu.VMEM((tokens, hidden), jnp.bfloat16),
            pltpu.VMEM((tokens, 128), jnp.float32),
            pltpu.VMEM((tokens, 128), jnp.float32),
        ],
        compiler_params=pltpu.CompilerParams(vmem_limit_bytes=8 * 1024 * 1024),
        cost_estimate=pl.CostEstimate(flops=tokens, bytes_accessed=tokens, transcendentals=0),
    )(*operands)


def sum_kernel(rows, keep, arrived, *outs):
    both = keep[...].astype(jnp.float32) + arrived[...].astype(jnp.float32)
    at = 0
    for out in outs:
        block, start = at // D, at % D
        out[...] = both[block * rows : (block + 1) * rows, start : start + out.shape[1]].astype(out.dtype)
        at += out.shape[1]


def sum_cores(keep, arrived, columns, kind, per):
    rows = keep.shape[0] // columns
    outs = [jax.ShapeDtypeStruct((rows, D // PARTS), kind)] * PARTS
    outs += [jax.ShapeDtypeStruct((rows, D // per), jnp.bfloat16)] * ((columns - 1) * per)
    sums = pl.pallas_call(
        functools.partial(sum_kernel, rows),
        out_shape=outs,
        in_specs=[pl.BlockSpec(memory_space=pltpu.VMEM)] * 2,
        out_specs=[pl.BlockSpec(memory_space=pltpu.VMEM)] * len(outs),
        compiler_params=pltpu.CompilerParams(vmem_limit_bytes=8 * 1024 * 1024),
        cost_estimate=pl.CostEstimate(flops=rows, bytes_accessed=rows, transcendentals=0),
    )(keep, arrived)
    return sums[:PARTS], [sums[PARTS + part :: per] for part in range(per)]


def pack_kernel(ranks, *refs):
    parts, out = refs[:-1], refs[-1]
    at = 0
    for part in parts:
        out[:, at : at + part.shape[1]] = part[...]
        at += part.shape[1]
    row = lax.broadcasted_iota(jnp.int32, (ranks.shape[0], 128), 0)
    marks = sum(jnp.where(row == m, ranks[m], 0) for m in range(ranks.shape[0]))
    out[:, at:] = marks.astype(jnp.float32).astype(jnp.bfloat16)


def pack_members(key_left, key_right, value_left, value_right, ranks):
    parts = (key_left, value_right, key_right, value_left)
    wide = sum(part.shape[1] for part in parts) + 128
    return pl.pallas_call(
        pack_kernel,
        out_shape=jax.ShapeDtypeStruct((ranks.shape[0], wide), jnp.bfloat16),
        in_specs=[pl.BlockSpec(memory_space=pltpu.SMEM)] + [pl.BlockSpec(memory_space=pltpu.VMEM)] * 4,
        out_specs=pl.BlockSpec(memory_space=pltpu.VMEM),
        compiler_params=pltpu.CompilerParams(vmem_limit_bytes=4 * 1024 * 1024),
        cost_estimate=pl.CostEstimate(flops=wide, bytes_accessed=wide, transcendentals=0),
    )(ranks, *parts)


def load_kernel(*refs):
    count = len(refs) // 2
    sems = refs[-1]
    copies = [pltpu.make_async_copy(refs[i], refs[count + i], sems.at[i]) for i in range(count)]
    for copy in copies:
        copy.start()
    for copy in copies:
        copy.wait()


def load(*arrays):
    size = sum(array.size * array.dtype.itemsize for array in arrays)
    return pl.pallas_call(
        load_kernel,
        out_shape=[jax.ShapeDtypeStruct(array.shape, array.dtype) for array in arrays],
        in_specs=[pl.BlockSpec(memory_space=pltpu.HBM)] * len(arrays),
        out_specs=[pl.BlockSpec(memory_space=pltpu.VMEM)] * len(arrays),
        scratch_shapes=[pltpu.SemaphoreType.DMA((len(arrays),))],
        compiler_params=pltpu.CompilerParams(vmem_limit_bytes=1024 * 1024),
        cost_estimate=pl.CostEstimate(flops=size // D, bytes_accessed=size // D, transcendentals=0),
    )(*arrays)


def update_kernel(fit_rows, piece, groups, hidden, count, *refs):
    packs, out, right = refs[:count], refs[-2], refs[-1]
    part, rows = D // groups, out.shape[0]

    def columns(start, size):
        at = pl.ds(pl.multiple_of(start, 128), size)
        return jnp.concatenate([ref[:, at].astype(jnp.float32) for ref in packs], 0)

    def split(array):
        everyone = array.shape[0]
        fitness = columns(packs[0].shape[1] - 128, 128)[:, :1] / (everyone - 1) - 0.5
        rest, terms = 2.0 / math.sqrt(everyone) * fitness * array, []
        for _ in range(3):
            terms.append(rest.astype(jnp.bfloat16).astype(jnp.float32))
            rest = rest - terms[-1]
        return jnp.concatenate(terms, 0).astype(jnp.bfloat16)

    def thrice(array):
        return jnp.concatenate([array] * 3, 0).astype(jnp.bfloat16)

    half = lax.axis_index("member") * part
    step = (piece * pl.num_programs(0) + pl.program_id(0)) * rows

    @pl.when(pl.program_id(0) == 0)
    def _():
        right[...] = thrice(columns(2 * D, hidden)) if fit_rows else split(columns(D + half, part))

    left = split(columns(half + step, rows)) if fit_rows else thrice(columns(2 * D + hidden + step, rows))
    out[...] = lax.dot_general(left, right[...], (((0,), (0,)), ((), ())), preferred_element_type=jnp.float32)


def update(fit_rows, packs, done, piece, groups, hidden):
    part = D // groups
    shape, rows = ((part, hidden), 256) if fit_rows else ((hidden, part), 128)
    rows = min(rows, shape[0] // PIECES)
    steps = shape[0] // rows // PIECES
    done = [] if done is None else [done]
    return pl.pallas_call(
        functools.partial(update_kernel, fit_rows, piece, groups, hidden, len(packs)),
        out_shape=jax.ShapeDtypeStruct(shape, jnp.float32),
        grid=(steps,),
        in_specs=[pl.BlockSpec(memory_space=pltpu.VMEM)] * len(packs) + [pl.BlockSpec(memory_space=pl.ANY)] * len(done),
        out_specs=pl.BlockSpec((rows, shape[1]), lambda i: (piece * steps + i, 0)),
        scratch_shapes=[pltpu.VMEM((3 * packs[0].shape[0] * len(packs), shape[1]), jnp.bfloat16)],
        input_output_aliases={len(packs): 0} if done else {},
        compiler_params=pltpu.CompilerParams(vmem_limit_bytes=12 * 1024 * 1024),
        cost_estimate=pl.CostEstimate(flops=rows, bytes_accessed=rows, transcendentals=0),
    )(*packs, *done)


def together(*values):
    return lax.optimization_barrier(values)


def local(
    tokens, key_weight, value_weight, shift_mix, key_left, key_right, value_left, value_right, ranks
):
    devices, groups = lax.axis_size("shard"), lax.axis_size("member")
    columns = devices // (PLANES * CORES)
    rows, hidden = tokens.shape[0], key_weight.shape[1]
    parts = [slice(i * D // PARTS, (i + 1) * D // PARTS) for i in range(PARTS)]

    def swap(array, bits):
        return lax.ppermute(array, "shard", [(i, i ^ bits) for i in range(devices)])

    def over_z(array, k):
        return swap(array, k * columns * CORES)

    def over_y(array):
        return [swap(array, j * CORES) for j in range(1, columns)]

    def over_cores(arrays):
        return [swap(array, 1) for array in arrays]

    def back_y(terms):
        return [swap(term, j * CORES) for j, term in enumerate(terms, 1)]

    def updates(fit_rows, packs, done, start, stop):
        for piece in range(start, stop):
            done = update(fit_rows, packs, done, piece, groups, hidden)
        return done

    def add(mine, arrived):
        return functools.reduce(lambda total, part: total + part.astype(jnp.float32), arrived, mine)

    def by_block(*blocks):
        return [list(block) for block in zip(*blocks)]

    def rounded(array):
        return array.astype(jnp.bfloat16)

    far, near, y0, c0 = over_z(tokens, 2), over_z(tokens, 1), over_y(tokens), over_cores([tokens])
    mix, key = together(shift_mix[None, :], key_weight)
    (key,) = load(key)
    near, y0, c0, key, value = together(near, y0, c0, key, value_weight)

    y1, cy0, c1 = over_y(near), over_cores(y0), over_cores([near])
    (value,) = load(value)
    far, y1, cy0, c1, key, value, left = together(far, y1, cy0, c1, key, value, key_left)

    def partial(k, own, other):
        return chunk(k, own, other, mix, key_left, key_right, value_left, value_right, key, value)

    pack = pack_members(left, key_right, value_left, value_right, ranks)
    packs = [pack] + [
        lax.ppermute(pack, "member", [(i, i ^ bits) for i in range(groups)]) for bits in range(1, groups)
    ]
    farthest, y2, c2, cy1 = over_z(far, 1), over_y(far), over_cores([far]), over_cores(y1)
    keep0, send0 = partial(0, [tokens] + y0, c0 + cy0)
    farthest, y2, c2, cy1, keep0, send0, packs = together(farthest, y2, c2, cy1, keep0, send0, packs)

    y3, c3, cy2 = over_y(farthest), over_cores([farthest]), over_cores(y2)
    keep1, send1 = partial(1, [near] + y1, c1 + cy1)
    far, keep1 = together(far, keep1)
    keep2, send2 = partial(2, [far] + y2, c2 + cy2)
    y3, c3, keep1, send1, keep2, send2 = together(y3, c3, keep1, send1, keep2, send2)

    cy3 = over_cores(y3)
    mine2, terms2 = sum_cores(keep2, *over_cores([send2]), columns, jnp.float32, PARTS)
    (other1,) = over_cores([send1])
    farthest, mine2, terms2 = together(farthest, mine2, terms2)
    back2a = back_y(terms2[0])
    keep3, send3 = partial(3, [farthest] + y3, c3 + cy3)
    back2a, other1, send0, keep3, send3 = together(back2a, other1, send0, keep3, send3)

    mine1, (terms1,) = sum_cores(keep1, other1, columns, jnp.bfloat16, 1)
    beside1 = [over_z(term, 1) for term in terms1]
    (back0,) = over_cores([send0])
    mine3, terms3 = sum_cores(keep3, *over_cores([send3]), columns, jnp.float32, PARTS)
    packs, mine3, terms3 = together(packs, mine3, terms3)
    back3 = back_y(terms3[0])
    key_update = updates(True, packs, None, 0, 2)
    back3, beside1, back0, rest3, key_update, mine1 = together(
        back3, beside1, back0, terms3[1], key_update, mine1
    )

    onward, mine1a = over_z(rounded(add(mine3[0], back3)), 1), over_z(mine1[0], 1)
    back3 = back_y(rest3)
    both = keep0.astype(jnp.float32) + back0.astype(jnp.float32)
    terms0 = [
        rounded(add(both[j * rows : (j + 1) * rows], [term])) for j, term in enumerate(beside1, 1)
    ]
    key_update = updates(True, packs, key_update, 2, 4)
    onward, back3, terms0, packs, rest2, key_update, mine1a, rest1 = together(
        onward, back3, terms0, packs, terms2[1], key_update, mine1a, mine1[1]
    )

    first = over_z(rounded(add(mine2[0], back2a + [onward])), 2)
    onward = over_z(rounded(add(mine3[1], back3)), 1)
    back2b = back_y(rest2)
    value_update = updates(False, packs, None, 0, 2)
    first, onward, back2b, value_update, packs, terms0, rest1 = together(
        first, onward, back2b, value_update, packs, terms0, rest1
    )

    second = over_z(rounded(add(mine2[1], back2b + [onward])), 2)
    back0, mine1b = back_y(terms0), over_z(rest1, 1)
    value_update = updates(False, packs, value_update, 2, 4)
    result = [
        add(both[:rows, at], [side, arrived] + [term[:, at] for term in back0])
        for at, side, arrived in zip(parts, (mine1a, mine1b), (first, second))
    ]
    return rounded(jnp.concatenate(result, 1)), key_update, value_update


def solution(mesh):
    placed = (
        P(("member", "shard"), None),
        P(None, "shard"),
        P("shard", None),
        P(),
        P("member", None),
        P("member", "shard"),
        P("member", "shard"),
        P("member", None),
        P("member"),
    )
    return jax.shard_map(
        local,
        mesh=mesh,
        in_specs=placed,
        out_specs=(P(("member", "shard"), None), P("member", "shard"), P("shard", "member")),
        check_vma=False,
    )
```

```python
import functools
import math

import jax
import jax.numpy as jnp
from jax import lax
from jax.experimental import pallas as pl
from jax.experimental.pallas import tpu as pltpu
from jax.sharding import PartitionSpec as P

D = 4096
FF = 16384
LEN = 64
PLANES = 4
CORES = 2
STEP = 1024
PIECES = 2


def chunk_kernel(k, rows, columns, *refs):
    own, other = refs[:columns], refs[columns : 2 * columns]
    mix, key_left, key_right, value_left, value_right, key, value = refs[2 * columns : 2 * columns + 7]
    keep, send, whole, natural, relative, natural_dots, dots = refs[2 * columns + 7 :]
    me = lax.axis_index("shard")
    core, y, plane = me % CORES, me // CORES % columns, me // (CORES * columns) ^ k
    tokens = rows * columns * CORES
    members = tokens // LEN

    def place(j, c):
        return pl.multiple_of(((y ^ j) * CORES + c) * rows, rows)

    def pick(array, member):
        at = lax.broadcasted_iota(jnp.int32, array.shape, 0) == member
        return jnp.sum(jnp.where(at, array.astype(jnp.float32), 0.0), 0, keepdims=True)

    for j in range(columns):
        whole[pl.ds(place(j, core), rows), :] = own[j][...]
        whole[pl.ds(place(j, 1 - core), rows), :] = other[j][...]

    inside = lax.broadcasted_iota(jnp.int32, (tokens, 1), 0) % LEN != 0
    total, along = None, [0.0] * members
    for start in range(0, D, STEP):
        at = slice(start, start + STEP)
        current = whole[:, at].astype(jnp.float32)
        previous = jnp.where(inside, pltpu.roll(current, 1, 0), 0.0)
        shifted = (current + (previous - current) * mix[:, at].astype(jnp.float32)).astype(jnp.bfloat16)
        part = jnp.dot(shifted, key[at, :], preferred_element_type=jnp.float32)
        total = part if total is None else total + part
        for m in range(members):
            wide = shifted[m * LEN : (m + 1) * LEN].astype(jnp.float32)
            products = wide * pick(key_left[:, at], plane * members + m)
            along[m] = along[m] + sum(products[:, i : i + 128] for i in range(0, STEP, 128))

    for m in range(members):
        at = slice(m * LEN, (m + 1) * LEN)
        dot = 0.5 / math.sqrt(D) * jnp.sum(along[m], 1, keepdims=True)
        hidden = total[at] + dot * pick(key_right[...], plane * members + m)
        keyed = jnp.square(jnp.maximum(hidden, 0.0)).astype(jnp.bfloat16)
        natural[at, :] = keyed
        dot = jnp.sum(keyed.astype(jnp.float32) * pick(value_left[...], plane * members + m), 1, keepdims=True)
        natural_dots[at, :] = jnp.broadcast_to(0.5 / math.sqrt(FF) * dot, (LEN, 128))

    cores = (core, 1 - core)
    for c in range(CORES):
        for j in range(columns):
            to = slice((c * columns + j) * rows, (c * columns + j + 1) * rows)
            relative[to, :] = natural[pl.ds(place(j, cores[c]), rows), :]
            dots[to, :] = natural_dots[pl.ds(place(j, cores[c]), rows), :]

    for start in range(0, D, STEP):
        at = slice(start, start + STEP)
        result = jnp.dot(relative[...], value[:, at], preferred_element_type=jnp.float32)
        for c, out in enumerate((keep, send)):
            for j in range(columns):
                to = slice((c * columns + j) * rows, (c * columns + j + 1) * rows)
                right = pick(value_right[:, at], plane * members + place(j, cores[c]) // LEN)
                out[j * rows : (j + 1) * rows, at] = (result[to] + dots[to, :1] * right).astype(jnp.bfloat16)


def chunk(k, own, other, mix, key_left, key_right, value_left, value_right, key, value):
    columns, rows = len(own), own[0].shape[0]
    hidden = key.shape[1]
    tokens = rows * columns * CORES
    operands = (*own, *other, mix, key_left, key_right, value_left, value_right, key, value)
    return pl.pallas_call(
        functools.partial(chunk_kernel, k, rows, columns),
        out_shape=[jax.ShapeDtypeStruct((columns * rows, D), jnp.bfloat16)] * 2,
        in_specs=[pl.BlockSpec(memory_space=pltpu.VMEM)] * len(operands),
        out_specs=[pl.BlockSpec(memory_space=pltpu.VMEM)] * 2,
        scratch_shapes=[
            pltpu.VMEM((tokens, D), jnp.bfloat16),
            pltpu.VMEM((tokens, hidden), jnp.bfloat16),
            pltpu.VMEM((tokens, hidden), jnp.bfloat16),
            pltpu.VMEM((tokens, 128), jnp.float32),
            pltpu.VMEM((tokens, 128), jnp.float32),
        ],
        compiler_params=pltpu.CompilerParams(vmem_limit_bytes=8 * 1024 * 1024),
        cost_estimate=pl.CostEstimate(flops=tokens, bytes_accessed=tokens, transcendentals=0),
    )(*operands)


def sum_kernel(rows, keep, arrived, *outs):
    both = keep[...].astype(jnp.float32) + arrived[...].astype(jnp.float32)
    at = 0
    for out in outs:
        out[...] = both[at : at + out.shape[0]].astype(out.dtype)
        at += out.shape[0]


def sum_cores(keep, arrived, columns, kind):
    rows = keep.shape[0] // columns
    outs = [jax.ShapeDtypeStruct((rows, D), k) for k in [kind] + [jnp.bfloat16] * (columns - 1)]
    return pl.pallas_call(
        functools.partial(sum_kernel, rows),
        out_shape=outs,
        in_specs=[pl.BlockSpec(memory_space=pltpu.VMEM)] * 2,
        out_specs=[pl.BlockSpec(memory_space=pltpu.VMEM)] * len(outs),
        compiler_params=pltpu.CompilerParams(vmem_limit_bytes=8 * 1024 * 1024),
        cost_estimate=pl.CostEstimate(flops=rows, bytes_accessed=rows, transcendentals=0),
    )(keep, arrived)


def pack_kernel(ranks, *refs):
    parts, out = refs[:-1], refs[-1]
    at = 0
    for part in parts:
        out[:, at : at + part.shape[1]] = part[...]
        at += part.shape[1]
    row = lax.broadcasted_iota(jnp.int32, (ranks.shape[0], 128), 0)
    marks = sum(jnp.where(row == m, ranks[m], 0) for m in range(ranks.shape[0]))
    out[:, at:] = marks.astype(jnp.float32).astype(jnp.bfloat16)


def pack_members(key_left, key_right, value_left, value_right, ranks):
    parts = (key_left, value_right, key_right, value_left)
    wide = sum(part.shape[1] for part in parts) + 128
    return pl.pallas_call(
        pack_kernel,
        out_shape=jax.ShapeDtypeStruct((ranks.shape[0], wide), jnp.bfloat16),
        in_specs=[pl.BlockSpec(memory_space=pltpu.SMEM)] + [pl.BlockSpec(memory_space=pltpu.VMEM)] * 4,
        out_specs=pl.BlockSpec(memory_space=pltpu.VMEM),
        compiler_params=pltpu.CompilerParams(vmem_limit_bytes=4 * 1024 * 1024),
        cost_estimate=pl.CostEstimate(flops=wide, bytes_accessed=wide, transcendentals=0),
    )(ranks, *parts)


def load_kernel(*refs):
    count = len(refs) // 2
    sems = refs[-1]
    copies = [pltpu.make_async_copy(refs[i], refs[count + i], sems.at[i]) for i in range(count)]
    for copy in copies:
        copy.start()
    for copy in copies:
        copy.wait()


def load(*arrays):
    size = sum(array.size * array.dtype.itemsize for array in arrays)
    return pl.pallas_call(
        load_kernel,
        out_shape=[jax.ShapeDtypeStruct(array.shape, array.dtype) for array in arrays],
        in_specs=[pl.BlockSpec(memory_space=pltpu.HBM)] * len(arrays),
        out_specs=[pl.BlockSpec(memory_space=pltpu.VMEM)] * len(arrays),
        scratch_shapes=[pltpu.SemaphoreType.DMA((len(arrays),))],
        compiler_params=pltpu.CompilerParams(vmem_limit_bytes=1024 * 1024),
        cost_estimate=pl.CostEstimate(flops=size // D, bytes_accessed=size // D, transcendentals=0),
    )(*arrays)


def update_kernel(fit_rows, piece, groups, hidden, count, *refs):
    packs, out, right = refs[:count], refs[-2], refs[-1]
    part, rows = D // groups, out.shape[0]

    def columns(start, size):
        at = pl.ds(pl.multiple_of(start, 128), size)
        return jnp.concatenate([ref[:, at].astype(jnp.float32) for ref in packs], 0)

    def split(array):
        everyone = array.shape[0]
        fitness = columns(packs[0].shape[1] - 128, 128)[:, :1] / (everyone - 1) - 0.5
        rest, terms = 2.0 / math.sqrt(everyone) * fitness * array, []
        for _ in range(3):
            terms.append(rest.astype(jnp.bfloat16).astype(jnp.float32))
            rest = rest - terms[-1]
        return jnp.concatenate(terms, 0).astype(jnp.bfloat16)

    def thrice(array):
        return jnp.concatenate([array] * 3, 0).astype(jnp.bfloat16)

    half = lax.axis_index("member") * part
    step = (piece * pl.num_programs(0) + pl.program_id(0)) * rows

    @pl.when(pl.program_id(0) == 0)
    def _():
        right[...] = thrice(columns(2 * D, hidden)) if fit_rows else split(columns(D + half, part))

    left = split(columns(half + step, rows)) if fit_rows else thrice(columns(2 * D + hidden + step, rows))
    out[...] = lax.dot_general(left, right[...], (((0,), (0,)), ((), ())), preferred_element_type=jnp.float32)


def update(fit_rows, packs, done, piece, groups, hidden):
    part = D // groups
    shape, rows = ((part, hidden), 256) if fit_rows else ((hidden, part), 128)
    rows = min(rows, shape[0] // PIECES)
    steps = shape[0] // rows // PIECES
    done = [] if done is None else [done]
    return pl.pallas_call(
        functools.partial(update_kernel, fit_rows, piece, groups, hidden, len(packs)),
        out_shape=jax.ShapeDtypeStruct(shape, jnp.float32),
        grid=(steps,),
        in_specs=[pl.BlockSpec(memory_space=pltpu.VMEM)] * len(packs) + [pl.BlockSpec(memory_space=pl.ANY)] * len(done),
        out_specs=pl.BlockSpec((rows, shape[1]), lambda i: (piece * steps + i, 0)),
        scratch_shapes=[pltpu.VMEM((3 * packs[0].shape[0] * len(packs), shape[1]), jnp.bfloat16)],
        input_output_aliases={len(packs): 0} if done else {},
        compiler_params=pltpu.CompilerParams(vmem_limit_bytes=12 * 1024 * 1024),
        cost_estimate=pl.CostEstimate(flops=rows, bytes_accessed=rows, transcendentals=0),
    )(*packs, *done)


def together(*values):
    return lax.optimization_barrier(values)


def local(
    tokens, key_weight, value_weight, shift_mix, key_left, key_right, value_left, value_right, ranks
):
    devices, groups = lax.axis_size("shard"), lax.axis_size("member")
    columns = devices // (PLANES * CORES)
    rows, hidden = tokens.shape[0], key_weight.shape[1]

    def swap(array, bits):
        return lax.ppermute(array, "shard", [(i, i ^ bits) for i in range(devices)])

    def over_z(array, k):
        return swap(array, k * columns * CORES)

    def over_y(array):
        return [swap(array, j * CORES) for j in range(1, columns)]

    def over_both(array):
        return [swap(array, (columns + j) * CORES) for j in range(1, columns)]

    def over_cores(arrays):
        return [swap(array, 1) for array in arrays]

    def back_y(terms):
        return [swap(term, j * CORES) for j, term in enumerate(terms, 1)]

    def updates(fit_rows, packs, done, start, stop):
        for piece in range(start, stop):
            done = update(fit_rows, packs, done, piece, groups, hidden)
        return done

    def add(mine, arrived):
        return functools.reduce(lambda total, part: total + part.astype(jnp.float32), arrived, mine)

    def by_block(*blocks):
        return [list(block) for block in zip(*blocks)]

    def rounded(array):
        return array.astype(jnp.bfloat16)

    far, near, y0, c0 = over_z(tokens, 2), over_z(tokens, 1), over_y(tokens), over_cores([tokens])
    mix, key = together(shift_mix[None, :], key_weight)
    (key,) = load(key)
    near, y0, c0, key, value, left = together(near, y0, c0, key, value_weight, key_left)

    y1, cy0, c1 = over_y(near), over_cores(y0), over_cores([near])
    (value,) = load(value)
    pack = pack_members(left, key_right, value_left, value_right, ranks)
    packs = [pack] + [
        lax.ppermute(pack, "member", [(i, i ^ bits) for i in range(groups)]) for bits in range(1, groups)
    ]
    far, y1, cy0, c1, key, value, packs = together(far, y1, cy0, c1, key, value, packs)

    def partial(k, own, other):
        return chunk(k, own, other, mix, key_left, key_right, value_left, value_right, key, value)

    farthest, y2, y3, c2, cy1 = over_z(far, 1), over_y(far), over_both(far), over_cores([far]), over_cores(y1)
    keep1, send1 = partial(1, [near] + y1, c1 + cy1)
    own, keep1 = together(tokens, keep1)
    keep0, send0 = partial(0, [own] + y0, c0 + cy0)
    packs, keep0 = together(packs, keep0)
    key_update = updates(True, packs, None, 0, 1)
    farthest, y2, y3, c2, keep1, send1, send0, key_update = together(
        farthest, y2, y3, c2, keep1, send1, send0, key_update
    )

    c3, cy3, cy2, other1 = over_cores([farthest]), over_cores(y3), over_cores(y2), over_cores([send1])
    keep3, send3 = partial(3, [farthest] + y3, c3 + cy3)
    cy2, other1, keep3, send3 = together(cy2, other1, keep3, send3)

    mine1, *terms1 = sum_cores(keep1, *other1, columns, jnp.bfloat16)
    beside1 = [over_z(term, 1) for term in terms1]
    mine3, *terms3 = sum_cores(keep3, *over_cores([send3]), columns, jnp.float32)
    far, mine3, terms3 = together(far, mine3, terms3)
    back3 = back_y(terms3)
    keep2, send2 = partial(2, [far] + y2, c2 + cy2)
    beside1, back3, keep2, send2, send0, packs, mine1 = together(
        beside1, back3, keep2, send2, send0, packs, mine1
    )

    onward = over_z(rounded(add(mine3, back3)), 1)
    other0, other2 = over_cores([send0, send2])
    mine2, *terms2 = sum_cores(keep2, other2, columns, jnp.float32)
    packs, mine2, terms2 = together(packs, mine2, terms2)
    back2 = back_y(terms2)
    key_update = updates(True, packs, key_update, 1, 2)
    onward, mine2, back2, other0, key_update, packs, mine1 = together(
        onward, mine2, back2, other0, key_update, packs, mine1
    )

    last = over_z(rounded(add(mine2, back2 + [onward])), 2)
    both = keep0.astype(jnp.float32) + other0.astype(jnp.float32)
    terms0 = [rounded(add(both[j * rows : (j + 1) * rows], [term])) for j, term in enumerate(beside1, 1)]
    back0, mine1 = back_y(terms0), over_z(mine1, 1)
    value_update = updates(False, packs, None, 0, 2)
    return rounded(add(both[:rows], [last, mine1] + back0)), key_update, value_update


def solution(mesh):
    placed = (
        P(("member", "shard"), None),
        P(None, "shard"),
        P("shard", None),
        P(),
        P("member", None),
        P("member", "shard"),
        P("member", "shard"),
        P("member", None),
        P("member"),
    )
    return jax.shard_map(
        local,
        mesh=mesh,
        in_specs=placed,
        out_specs=(P(("member", "shard"), None), P("member", "shard"), P("shard", "member")),
        check_vma=False,
    )
```

```python
import functools
import math

import jax
import jax.numpy as jnp
from jax import lax
from jax.experimental import pallas as pl
from jax.experimental.pallas import tpu as pltpu
from jax.sharding import PartitionSpec as P

D = 4096
FF = 16384
LEN = 64
PLANES = 4
CORES = 2
STEP = 1024
PIECES = 4


def chunk_kernel(k, rows, columns, *refs):
    own, other = refs[:columns], refs[columns : 2 * columns]
    mix, key_left, key_right, value_left, value_right, key, value = refs[2 * columns : 2 * columns + 7]
    keep, send, whole, natural, relative, natural_dots, dots = refs[2 * columns + 7 :]
    me = lax.axis_index("shard")
    core, y, plane = me % CORES, me // CORES % columns, me // (CORES * columns) ^ k
    tokens = rows * columns * CORES
    members = tokens // LEN

    def place(j, c):
        return pl.multiple_of(((y ^ j) * CORES + c) * rows, rows)

    def pick(array, member):
        at = lax.broadcasted_iota(jnp.int32, array.shape, 0) == member
        return jnp.sum(jnp.where(at, array.astype(jnp.float32), 0.0), 0, keepdims=True)

    for j in range(columns):
        whole[pl.ds(place(j, core), rows), :] = own[j][...]
        whole[pl.ds(place(j, 1 - core), rows), :] = other[j][...]

    inside = lax.broadcasted_iota(jnp.int32, (tokens, 1), 0) % LEN != 0
    total, along = None, [0.0] * members
    for start in range(0, D, STEP):
        at = slice(start, start + STEP)
        current = whole[:, at].astype(jnp.float32)
        previous = jnp.where(inside, pltpu.roll(current, 1, 0), 0.0)
        shifted = (current + (previous - current) * mix[:, at].astype(jnp.float32)).astype(jnp.bfloat16)
        part = jnp.dot(shifted, key[at, :], preferred_element_type=jnp.float32)
        total = part if total is None else total + part
        for m in range(members):
            wide = shifted[m * LEN : (m + 1) * LEN].astype(jnp.float32)
            products = wide * pick(key_left[:, at], plane * members + m)
            along[m] = along[m] + sum(products[:, i : i + 128] for i in range(0, STEP, 128))

    for m in range(members):
        at = slice(m * LEN, (m + 1) * LEN)
        dot = 0.5 / math.sqrt(D) * jnp.sum(along[m], 1, keepdims=True)
        hidden = total[at] + dot * pick(key_right[...], plane * members + m)
        keyed = jnp.square(jnp.maximum(hidden, 0.0)).astype(jnp.bfloat16)
        natural[at, :] = keyed
        dot = jnp.sum(keyed.astype(jnp.float32) * pick(value_left[...], plane * members + m), 1, keepdims=True)
        natural_dots[at, :] = jnp.broadcast_to(0.5 / math.sqrt(FF) * dot, (LEN, 128))

    cores = (core, 1 - core)
    for c in range(CORES):
        for j in range(columns):
            to = slice((c * columns + j) * rows, (c * columns + j + 1) * rows)
            relative[to, :] = natural[pl.ds(place(j, cores[c]), rows), :]
            dots[to, :] = natural_dots[pl.ds(place(j, cores[c]), rows), :]

    for start in range(0, D, STEP):
        at = slice(start, start + STEP)
        result = jnp.dot(relative[...], value[:, at], preferred_element_type=jnp.float32)
        for c, out in enumerate((keep, send)):
            for j in range(columns):
                to = slice((c * columns + j) * rows, (c * columns + j + 1) * rows)
                right = pick(value_right[:, at], plane * members + place(j, cores[c]) // LEN)
                out[j * rows : (j + 1) * rows, at] = (result[to] + dots[to, :1] * right).astype(jnp.bfloat16)


def chunk(k, own, other, mix, key_left, key_right, value_left, value_right, key, value):
    columns, rows = len(own), own[0].shape[0]
    hidden = key.shape[1]
    tokens = rows * columns * CORES
    operands = (*own, *other, mix, key_left, key_right, value_left, value_right, key, value)
    return pl.pallas_call(
        functools.partial(chunk_kernel, k, rows, columns),
        out_shape=[jax.ShapeDtypeStruct((columns * rows, D), jnp.bfloat16)] * 2,
        in_specs=[pl.BlockSpec(memory_space=pltpu.VMEM)] * len(operands),
        out_specs=[pl.BlockSpec(memory_space=pltpu.VMEM)] * 2,
        scratch_shapes=[
            pltpu.VMEM((tokens, D), jnp.bfloat16),
            pltpu.VMEM((tokens, hidden), jnp.bfloat16),
            pltpu.VMEM((tokens, hidden), jnp.bfloat16),
            pltpu.VMEM((tokens, 128), jnp.float32),
            pltpu.VMEM((tokens, 128), jnp.float32),
        ],
        compiler_params=pltpu.CompilerParams(vmem_limit_bytes=8 * 1024 * 1024),
        cost_estimate=pl.CostEstimate(flops=tokens, bytes_accessed=tokens, transcendentals=0),
    )(*operands)


def sum_kernel(rows, keep, arrived, *outs):
    both = keep[...].astype(jnp.float32) + arrived[...].astype(jnp.float32)
    at = 0
    for out in outs:
        out[...] = both[at : at + out.shape[0]].astype(out.dtype)
        at += out.shape[0]


def sum_cores(keep, arrived, columns, kind):
    rows = keep.shape[0] // columns
    outs = [jax.ShapeDtypeStruct((rows, D), k) for k in [kind] + [jnp.bfloat16] * (columns - 1)]
    return pl.pallas_call(
        functools.partial(sum_kernel, rows),
        out_shape=outs,
        in_specs=[pl.BlockSpec(memory_space=pltpu.VMEM)] * 2,
        out_specs=[pl.BlockSpec(memory_space=pltpu.VMEM)] * len(outs),
        compiler_params=pltpu.CompilerParams(vmem_limit_bytes=8 * 1024 * 1024),
        cost_estimate=pl.CostEstimate(flops=rows, bytes_accessed=rows, transcendentals=0),
    )(keep, arrived)


def pack_kernel(ranks, *refs):
    parts, out = refs[:-1], refs[-1]
    at = 0
    for part in parts:
        out[:, at : at + part.shape[1]] = part[...]
        at += part.shape[1]
    row = lax.broadcasted_iota(jnp.int32, (ranks.shape[0], 128), 0)
    marks = sum(jnp.where(row == m, ranks[m], 0) for m in range(ranks.shape[0]))
    out[:, at:] = marks.astype(jnp.float32).astype(jnp.bfloat16)


def pack_members(key_left, key_right, value_left, value_right, ranks):
    parts = (key_left, value_right, key_right, value_left)
    wide = sum(part.shape[1] for part in parts) + 128
    return pl.pallas_call(
        pack_kernel,
        out_shape=jax.ShapeDtypeStruct((ranks.shape[0], wide), jnp.bfloat16),
        in_specs=[pl.BlockSpec(memory_space=pltpu.SMEM)] + [pl.BlockSpec(memory_space=pltpu.VMEM)] * 4,
        out_specs=pl.BlockSpec(memory_space=pltpu.VMEM),
        compiler_params=pltpu.CompilerParams(vmem_limit_bytes=4 * 1024 * 1024),
        cost_estimate=pl.CostEstimate(flops=wide, bytes_accessed=wide, transcendentals=0),
    )(ranks, *parts)


def load_kernel(*refs):
    count = len(refs) // 2
    sems = refs[-1]
    copies = [pltpu.make_async_copy(refs[i], refs[count + i], sems.at[i]) for i in range(count)]
    for copy in copies:
        copy.start()
    for copy in copies:
        copy.wait()


def load(*arrays):
    size = sum(array.size * array.dtype.itemsize for array in arrays)
    return pl.pallas_call(
        load_kernel,
        out_shape=[jax.ShapeDtypeStruct(array.shape, array.dtype) for array in arrays],
        in_specs=[pl.BlockSpec(memory_space=pltpu.HBM)] * len(arrays),
        out_specs=[pl.BlockSpec(memory_space=pltpu.VMEM)] * len(arrays),
        scratch_shapes=[pltpu.SemaphoreType.DMA((len(arrays),))],
        compiler_params=pltpu.CompilerParams(vmem_limit_bytes=1024 * 1024),
        cost_estimate=pl.CostEstimate(flops=size // D, bytes_accessed=size // D, transcendentals=0),
    )(*arrays)


def update_kernel(fit_rows, piece, groups, hidden, count, *refs):
    packs, out, right = refs[:count], refs[-2], refs[-1]
    part, rows = D // groups, out.shape[0]

    def columns(start, size):
        at = pl.ds(pl.multiple_of(start, 128), size)
        return jnp.concatenate([ref[:, at].astype(jnp.float32) for ref in packs], 0)

    def split(array):
        everyone = array.shape[0]
        fitness = columns(packs[0].shape[1] - 128, 128)[:, :1] / (everyone - 1) - 0.5
        rest, terms = 2.0 / math.sqrt(everyone) * fitness * array, []
        for _ in range(3):
            terms.append(rest.astype(jnp.bfloat16).astype(jnp.float32))
            rest = rest - terms[-1]
        return jnp.concatenate(terms, 0).astype(jnp.bfloat16)

    def thrice(array):
        return jnp.concatenate([array] * 3, 0).astype(jnp.bfloat16)

    half = lax.axis_index("member") * part
    step = (piece * pl.num_programs(0) + pl.program_id(0)) * rows

    @pl.when(pl.program_id(0) == 0)
    def _():
        right[...] = thrice(columns(2 * D, hidden)) if fit_rows else split(columns(D + half, part))

    left = split(columns(half + step, rows)) if fit_rows else thrice(columns(2 * D + hidden + step, rows))
    out[...] = lax.dot_general(left, right[...], (((0,), (0,)), ((), ())), preferred_element_type=jnp.float32)


def update(fit_rows, packs, done, piece, groups, hidden):
    part = D // groups
    shape, rows = ((part, hidden), 256) if fit_rows else ((hidden, part), 128)
    rows = min(rows, shape[0] // PIECES)
    steps = shape[0] // rows // PIECES
    done = [] if done is None else [done]
    return pl.pallas_call(
        functools.partial(update_kernel, fit_rows, piece, groups, hidden, len(packs)),
        out_shape=jax.ShapeDtypeStruct(shape, jnp.float32),
        grid=(steps,),
        in_specs=[pl.BlockSpec(memory_space=pltpu.VMEM)] * len(packs) + [pl.BlockSpec(memory_space=pl.ANY)] * len(done),
        out_specs=pl.BlockSpec((rows, shape[1]), lambda i: (piece * steps + i, 0)),
        scratch_shapes=[pltpu.VMEM((3 * packs[0].shape[0] * len(packs), shape[1]), jnp.bfloat16)],
        input_output_aliases={len(packs): 0} if done else {},
        compiler_params=pltpu.CompilerParams(vmem_limit_bytes=12 * 1024 * 1024),
        cost_estimate=pl.CostEstimate(flops=rows, bytes_accessed=rows, transcendentals=0),
    )(*packs, *done)


def together(*values):
    return lax.optimization_barrier(values)


def local(
    tokens, key_weight, value_weight, shift_mix, key_left, key_right, value_left, value_right, ranks
):
    devices, groups = lax.axis_size("shard"), lax.axis_size("member")
    columns = devices // (PLANES * CORES)
    rows, hidden = tokens.shape[0], key_weight.shape[1]

    def swap(array, bits):
        return lax.ppermute(array, "shard", [(i, i ^ bits) for i in range(devices)])

    def over_z(array, k):
        return swap(array, k * columns * CORES)

    def over_y(array):
        return [swap(array, j * CORES) for j in range(1, columns)]

    def over_both(array):
        return [swap(array, (columns + j) * CORES) for j in range(1, columns)]

    def over_cores(arrays):
        return [swap(array, 1) for array in arrays]

    def back_y(terms):
        return [swap(term, j * CORES) for j, term in enumerate(terms, 1)]

    def updates(fit_rows, packs, done, start, stop):
        for piece in range(start, stop):
            done = update(fit_rows, packs, done, piece, groups, hidden)
        return done

    def add(mine, arrived):
        return functools.reduce(lambda total, part: total + part.astype(jnp.float32), arrived, mine)

    def by_block(*blocks):
        return [list(block) for block in zip(*blocks)]

    def rounded(array):
        return array.astype(jnp.bfloat16)

    far, near, y0, c0 = over_z(tokens, 2), over_z(tokens, 1), over_y(tokens), over_cores([tokens])
    near, y0, c0, mix, key = together(near, y0, c0, shift_mix[None, :], key_weight)

    y1, cy0, c1 = over_y(near), over_cores(y0), over_cores([near])
    (key,) = load(key)
    far, y1, cy0, c1, key, value, left = together(far, y1, cy0, c1, key, value_weight, key_left)

    (value,) = load(value)
    pack = pack_members(left, key_right, value_left, value_right, ranks)
    packs = [pack] + [
        lax.ppermute(pack, "member", [(i, i ^ bits) for i in range(groups)]) for bits in range(1, groups)
    ]

    def partial(k, own, other):
        return chunk(k, own, other, mix, key_left, key_right, value_left, value_right, key, value)

    farthest, y2, y3, c2, cy1 = over_z(far, 1), over_y(far), over_both(far), over_cores([far]), over_cores(y1)
    keep1, send1 = partial(1, [near] + y1, c1 + cy1)
    own, keep1 = together(tokens, keep1)
    keep0, send0 = partial(0, [own] + y0, c0 + cy0)
    packs, keep0 = together(packs, keep0)
    key_update = updates(True, packs, None, 0, 1)
    farthest, y2, y3, c2, keep1, send1, send0, key_update = together(
        farthest, y2, y3, c2, keep1, send1, send0, key_update
    )

    c3, cy3, cy2, other1 = over_cores([farthest]), over_cores(y3), over_cores(y2), over_cores([send1])
    keep3, send3 = partial(3, [farthest] + y3, c3 + cy3)
    cy2, other1, keep3, send3 = together(cy2, other1, keep3, send3)

    mine1, *terms1 = sum_cores(keep1, *other1, columns, jnp.bfloat16)
    beside1 = [over_z(term, 1) for term in terms1]
    mine3, *terms3 = sum_cores(keep3, *over_cores([send3]), columns, jnp.float32)
    far, mine3, terms3 = together(far, mine3, terms3)
    back3 = back_y(terms3)
    keep2, send2 = partial(2, [far] + y2, c2 + cy2)
    packs, keep2 = together(packs, keep2)
    key_update = updates(True, packs, key_update, 1, 2)
    beside1, back3, keep2, send2, send0, packs, mine1, key_update = together(
        beside1, back3, keep2, send2, send0, packs, mine1, key_update
    )

    onward = over_z(rounded(add(mine3, back3)), 1)
    other0, other2 = over_cores([send0, send2])
    mine2, *terms2 = sum_cores(keep2, other2, columns, jnp.float32)
    packs, mine2, terms2 = together(packs, mine2, terms2)
    back2 = back_y(terms2)
    key_update = updates(True, packs, key_update, 2, 4)
    onward, mine2, back2, other0, key_update, packs, mine1 = together(
        onward, mine2, back2, other0, key_update, packs, mine1
    )

    last = over_z(rounded(add(mine2, back2 + [onward])), 2)
    both = keep0.astype(jnp.float32) + other0.astype(jnp.float32)
    terms0 = [rounded(add(both[j * rows : (j + 1) * rows], [term])) for j, term in enumerate(beside1, 1)]
    back0, mine1 = back_y(terms0), over_z(mine1, 1)
    value_update = updates(False, packs, None, 0, 4)
    return rounded(add(both[:rows], [last, mine1] + back0)), key_update, value_update


def solution(mesh):
    placed = (
        P(("member", "shard"), None),
        P(None, "shard"),
        P("shard", None),
        P(),
        P("member", None),
        P("member", "shard"),
        P("member", "shard"),
        P("member", None),
        P("member"),
    )
    return jax.shard_map(
        local,
        mesh=mesh,
        in_specs=placed,
        out_specs=(P(("member", "shard"), None), P("member", "shard"), P("shard", "member")),
        check_vma=False,
    )
```

```python
import functools
import math

import jax
import jax.numpy as jnp
from jax import lax
from jax.experimental import pallas as pl
from jax.experimental.pallas import tpu as pltpu
from jax.sharding import PartitionSpec as P

D = 4096
FF = 16384
LEN = 64
PLANES = 4
CORES = 2
STEP = 1024
PIECES = 4


def chunk_kernel(k, rows, columns, *refs):
    own, other = refs[:columns], refs[columns : 2 * columns]
    mix, key_left, key_right, value_left, value_right, key, value = refs[2 * columns : 2 * columns + 7]
    keep, send, whole, natural, relative, natural_dots, dots = refs[2 * columns + 7 :]
    me = lax.axis_index("shard")
    core, y, plane = me % CORES, me // CORES % columns, me // (CORES * columns) ^ k
    tokens = rows * columns * CORES
    members = tokens // LEN

    def place(j, c):
        return pl.multiple_of(((y ^ j) * CORES + c) * rows, rows)

    def pick(array, member):
        at = lax.broadcasted_iota(jnp.int32, array.shape, 0) == member
        return jnp.sum(jnp.where(at, array.astype(jnp.float32), 0.0), 0, keepdims=True)

    for j in range(columns):
        whole[pl.ds(place(j, core), rows), :] = own[j][...]
        whole[pl.ds(place(j, 1 - core), rows), :] = other[j][...]

    inside = lax.broadcasted_iota(jnp.int32, (tokens, 1), 0) % LEN != 0
    total, along = None, [0.0] * members
    for start in range(0, D, STEP):
        at = slice(start, start + STEP)
        current = whole[:, at].astype(jnp.float32)
        previous = jnp.where(inside, pltpu.roll(current, 1, 0), 0.0)
        shifted = (current + (previous - current) * mix[:, at].astype(jnp.float32)).astype(jnp.bfloat16)
        part = jnp.dot(shifted, key[at, :], preferred_element_type=jnp.float32)
        total = part if total is None else total + part
        for m in range(members):
            wide = shifted[m * LEN : (m + 1) * LEN].astype(jnp.float32)
            products = wide * pick(key_left[:, at], plane * members + m)
            along[m] = along[m] + sum(products[:, i : i + 128] for i in range(0, STEP, 128))

    for m in range(members):
        at = slice(m * LEN, (m + 1) * LEN)
        dot = 0.5 / math.sqrt(D) * jnp.sum(along[m], 1, keepdims=True)
        hidden = total[at] + dot * pick(key_right[...], plane * members + m)
        keyed = jnp.square(jnp.maximum(hidden, 0.0)).astype(jnp.bfloat16)
        natural[at, :] = keyed
        dot = jnp.sum(keyed.astype(jnp.float32) * pick(value_left[...], plane * members + m), 1, keepdims=True)
        natural_dots[at, :] = jnp.broadcast_to(0.5 / math.sqrt(FF) * dot, (LEN, 128))

    cores = (core, 1 - core)
    for c in range(CORES):
        for j in range(columns):
            to = slice((c * columns + j) * rows, (c * columns + j + 1) * rows)
            relative[to, :] = natural[pl.ds(place(j, cores[c]), rows), :]
            dots[to, :] = natural_dots[pl.ds(place(j, cores[c]), rows), :]

    for start in range(0, D, STEP):
        at = slice(start, start + STEP)
        result = jnp.dot(relative[...], value[:, at], preferred_element_type=jnp.float32)
        for c, out in enumerate((keep, send)):
            for j in range(columns):
                to = slice((c * columns + j) * rows, (c * columns + j + 1) * rows)
                right = pick(value_right[:, at], plane * members + place(j, cores[c]) // LEN)
                out[j * rows : (j + 1) * rows, at] = (result[to] + dots[to, :1] * right).astype(jnp.bfloat16)


def chunk(k, own, other, mix, key_left, key_right, value_left, value_right, key, value):
    columns, rows = len(own), own[0].shape[0]
    hidden = key.shape[1]
    tokens = rows * columns * CORES
    operands = (*own, *other, mix, key_left, key_right, value_left, value_right, key, value)
    return pl.pallas_call(
        functools.partial(chunk_kernel, k, rows, columns),
        out_shape=[jax.ShapeDtypeStruct((columns * rows, D), jnp.bfloat16)] * 2,
        in_specs=[pl.BlockSpec(memory_space=pltpu.VMEM)] * len(operands),
        out_specs=[pl.BlockSpec(memory_space=pltpu.VMEM)] * 2,
        scratch_shapes=[
            pltpu.VMEM((tokens, D), jnp.bfloat16),
            pltpu.VMEM((tokens, hidden), jnp.bfloat16),
            pltpu.VMEM((tokens, hidden), jnp.bfloat16),
            pltpu.VMEM((tokens, 128), jnp.float32),
            pltpu.VMEM((tokens, 128), jnp.float32),
        ],
        compiler_params=pltpu.CompilerParams(vmem_limit_bytes=8 * 1024 * 1024),
        cost_estimate=pl.CostEstimate(flops=tokens, bytes_accessed=tokens, transcendentals=0),
    )(*operands)


def sum_kernel(rows, keep, arrived, *outs):
    both = keep[...].astype(jnp.float32) + arrived[...].astype(jnp.float32)
    at = 0
    for out in outs:
        out[...] = both[at : at + out.shape[0]].astype(out.dtype)
        at += out.shape[0]


def sum_cores(keep, arrived, columns, kind):
    rows = keep.shape[0] // columns
    outs = [jax.ShapeDtypeStruct((rows, D), k) for k in [kind] + [jnp.bfloat16] * (columns - 1)]
    return pl.pallas_call(
        functools.partial(sum_kernel, rows),
        out_shape=outs,
        in_specs=[pl.BlockSpec(memory_space=pltpu.VMEM)] * 2,
        out_specs=[pl.BlockSpec(memory_space=pltpu.VMEM)] * len(outs),
        compiler_params=pltpu.CompilerParams(vmem_limit_bytes=8 * 1024 * 1024),
        cost_estimate=pl.CostEstimate(flops=rows, bytes_accessed=rows, transcendentals=0),
    )(keep, arrived)


def pack_kernel(ranks, *refs):
    parts, out = refs[:-1], refs[-1]
    at = 0
    for part in parts:
        out[:, at : at + part.shape[1]] = part[...]
        at += part.shape[1]
    row = lax.broadcasted_iota(jnp.int32, (ranks.shape[0], 128), 0)
    marks = sum(jnp.where(row == m, ranks[m], 0) for m in range(ranks.shape[0]))
    out[:, at:] = marks.astype(jnp.float32).astype(jnp.bfloat16)


def pack_members(key_left, key_right, value_left, value_right, ranks):
    parts = (key_left, value_right, key_right, value_left)
    wide = sum(part.shape[1] for part in parts) + 128
    return pl.pallas_call(
        pack_kernel,
        out_shape=jax.ShapeDtypeStruct((ranks.shape[0], wide), jnp.bfloat16),
        in_specs=[pl.BlockSpec(memory_space=pltpu.SMEM)] + [pl.BlockSpec(memory_space=pltpu.VMEM)] * 4,
        out_specs=pl.BlockSpec(memory_space=pltpu.VMEM),
        compiler_params=pltpu.CompilerParams(vmem_limit_bytes=4 * 1024 * 1024),
        cost_estimate=pl.CostEstimate(flops=wide, bytes_accessed=wide, transcendentals=0),
    )(ranks, *parts)


def load_kernel(*refs):
    count = len(refs) // 2
    sems = refs[-1]
    copies = [pltpu.make_async_copy(refs[i], refs[count + i], sems.at[i]) for i in range(count)]
    for copy in copies:
        copy.start()
    for copy in copies:
        copy.wait()


def load(*arrays):
    size = sum(array.size * array.dtype.itemsize for array in arrays)
    return pl.pallas_call(
        load_kernel,
        out_shape=[jax.ShapeDtypeStruct(array.shape, array.dtype) for array in arrays],
        in_specs=[pl.BlockSpec(memory_space=pltpu.HBM)] * len(arrays),
        out_specs=[pl.BlockSpec(memory_space=pltpu.VMEM)] * len(arrays),
        scratch_shapes=[pltpu.SemaphoreType.DMA((len(arrays),))],
        compiler_params=pltpu.CompilerParams(vmem_limit_bytes=1024 * 1024),
        cost_estimate=pl.CostEstimate(flops=size // D, bytes_accessed=size // D, transcendentals=0),
    )(*arrays)


def update_kernel(fit_rows, piece, groups, hidden, count, *refs):
    packs, out, right = refs[:count], refs[-2], refs[-1]
    part, rows = D // groups, out.shape[0]

    def columns(start, size):
        at = pl.ds(pl.multiple_of(start, 128), size)
        return jnp.concatenate([ref[:, at].astype(jnp.float32) for ref in packs], 0)

    def split(array):
        everyone = array.shape[0]
        fitness = columns(packs[0].shape[1] - 128, 128)[:, :1] / (everyone - 1) - 0.5
        rest, terms = 2.0 / math.sqrt(everyone) * fitness * array, []
        for _ in range(3):
            terms.append(rest.astype(jnp.bfloat16).astype(jnp.float32))
            rest = rest - terms[-1]
        return jnp.concatenate(terms, 0).astype(jnp.bfloat16)

    def thrice(array):
        return jnp.concatenate([array] * 3, 0).astype(jnp.bfloat16)

    half = lax.axis_index("member") * part
    step = (piece * pl.num_programs(0) + pl.program_id(0)) * rows

    @pl.when(pl.program_id(0) == 0)
    def _():
        right[...] = thrice(columns(2 * D, hidden)) if fit_rows else split(columns(D + half, part))

    left = split(columns(half + step, rows)) if fit_rows else thrice(columns(2 * D + hidden + step, rows))
    out[...] = lax.dot_general(left, right[...], (((0,), (0,)), ((), ())), preferred_element_type=jnp.float32)


def update(fit_rows, packs, done, piece, groups, hidden):
    part = D // groups
    shape, rows = ((part, hidden), 256) if fit_rows else ((hidden, part), 128)
    rows = min(rows, shape[0] // PIECES)
    steps = shape[0] // rows // PIECES
    done = [] if done is None else [done]
    return pl.pallas_call(
        functools.partial(update_kernel, fit_rows, piece, groups, hidden, len(packs)),
        out_shape=jax.ShapeDtypeStruct(shape, jnp.float32),
        grid=(steps,),
        in_specs=[pl.BlockSpec(memory_space=pltpu.VMEM)] * len(packs) + [pl.BlockSpec(memory_space=pl.ANY)] * len(done),
        out_specs=pl.BlockSpec((rows, shape[1]), lambda i: (piece * steps + i, 0)),
        scratch_shapes=[pltpu.VMEM((3 * packs[0].shape[0] * len(packs), shape[1]), jnp.bfloat16)],
        input_output_aliases={len(packs): 0} if done else {},
        compiler_params=pltpu.CompilerParams(vmem_limit_bytes=12 * 1024 * 1024),
        cost_estimate=pl.CostEstimate(flops=rows, bytes_accessed=rows, transcendentals=0),
    )(*packs, *done)


def together(*values):
    return lax.optimization_barrier(values)


def local(
    tokens, key_weight, value_weight, shift_mix, key_left, key_right, value_left, value_right, ranks
):
    devices, groups = lax.axis_size("shard"), lax.axis_size("member")
    columns = devices // (PLANES * CORES)
    rows, hidden = tokens.shape[0], key_weight.shape[1]

    def swap(array, bits):
        return lax.ppermute(array, "shard", [(i, i ^ bits) for i in range(devices)])

    def over_z(array, k):
        return swap(array, k * columns * CORES)

    def over_y(array):
        return [swap(array, j * CORES) for j in range(1, columns)]

    def over_both(array):
        return [swap(array, (columns + j) * CORES) for j in range(1, columns)]

    def over_cores(arrays):
        return [swap(array, 1) for array in arrays]

    def back_y(terms):
        return [swap(term, j * CORES) for j, term in enumerate(terms, 1)]

    def updates(fit_rows, packs, done, start, stop):
        for piece in range(start, stop):
            done = update(fit_rows, packs, done, piece, groups, hidden)
        return done

    def add(mine, arrived):
        return functools.reduce(lambda total, part: total + part.astype(jnp.float32), arrived, mine)

    def by_block(*blocks):
        return [list(block) for block in zip(*blocks)]

    def rounded(array):
        return array.astype(jnp.bfloat16)

    far, near, y0, c0 = over_z(tokens, 2), over_z(tokens, 1), over_y(tokens), over_cores([tokens])
    near, y0, c0, mix, key = together(near, y0, c0, shift_mix[None, :], key_weight)

    y1, cy0, c1 = over_y(near), over_cores(y0), over_cores([near])
    (key,) = load(key)
    far, y1, cy0, c1, key, value, left = together(far, y1, cy0, c1, key, value_weight, key_left)

    (value,) = load(value)
    pack = pack_members(left, key_right, value_left, value_right, ranks)
    packs = [pack] + [
        lax.ppermute(pack, "member", [(i, i ^ bits) for i in range(groups)]) for bits in range(1, groups)
    ]

    def partial(k, own, other):
        return chunk(k, own, other, mix, key_left, key_right, value_left, value_right, key, value)

    farthest, y2, y3, c2, cy1 = over_z(far, 1), over_y(far), over_both(far), over_cores([far]), over_cores(y1)
    keep1, send1 = partial(1, [near] + y1, c1 + cy1)
    own, keep1 = together(tokens, keep1)
    keep0, send0 = partial(0, [own] + y0, c0 + cy0)
    packs, keep0 = together(packs, keep0)
    key_update = updates(True, packs, None, 0, 1)
    farthest, y2, y3, c2, keep1, send1, send0, key_update = together(
        farthest, y2, y3, c2, keep1, send1, send0, key_update
    )

    c3, cy3, cy2, other1 = over_cores([farthest]), over_cores(y3), over_cores(y2), over_cores([send1])
    keep3, send3 = partial(3, [farthest] + y3, c3 + cy3)
    cy2, other1, keep3, send3 = together(cy2, other1, keep3, send3)

    mine1, *terms1 = sum_cores(keep1, *other1, columns, jnp.bfloat16)
    beside1 = [over_z(term, 1) for term in terms1]
    mine3, *terms3 = sum_cores(keep3, *over_cores([send3]), columns, jnp.float32)
    far, mine3, terms3 = together(far, mine3, terms3)
    back3 = back_y(terms3)
    keep2, send2 = partial(2, [far] + y2, c2 + cy2)
    packs, keep2 = together(packs, keep2)
    key_update = updates(True, packs, key_update, 1, 2)
    beside1, back3, keep2, send2, send0, packs, mine1, key_update = together(
        beside1, back3, keep2, send2, send0, packs, mine1, key_update
    )

    onward, early = over_z(rounded(add(mine3, back3)), 1), over_z(mine1[:, :STEP], 1)
    other0, other2 = over_cores([send0, send2])
    mine2, *terms2 = sum_cores(keep2, other2, columns, jnp.float32)
    packs, mine2, terms2 = together(packs, mine2, terms2)
    back2 = back_y(terms2)
    key_update = updates(True, packs, key_update, 2, 4)
    onward, mine2, back2, other0, key_update, packs, mine1, early = together(
        onward, mine2, back2, other0, key_update, packs, mine1, early
    )

    last = over_z(rounded(add(mine2, back2 + [onward])), 2)
    both = keep0.astype(jnp.float32) + other0.astype(jnp.float32)
    terms0 = [rounded(add(both[j * rows : (j + 1) * rows], [term])) for j, term in enumerate(beside1, 1)]
    back0, mine1 = back_y(terms0), jnp.concatenate([early, over_z(mine1[:, STEP:], 1)], 1)
    value_update = updates(False, packs, None, 0, 4)
    return rounded(add(both[:rows], [last, mine1] + back0)), key_update, value_update


def solution(mesh):
    placed = (
        P(("member", "shard"), None),
        P(None, "shard"),
        P("shard", None),
        P(),
        P("member", None),
        P("member", "shard"),
        P("member", "shard"),
        P("member", None),
        P("member"),
    )
    return jax.shard_map(
        local,
        mesh=mesh,
        in_specs=placed,
        out_specs=(P(("member", "shard"), None), P("member", "shard"), P("shard", "member")),
        check_vma=False,
    )
```

```python
import functools
import math

import jax
import jax.numpy as jnp
from jax import lax
from jax.experimental import pallas as pl
from jax.experimental.pallas import tpu as pltpu
from jax.sharding import PartitionSpec as P

D = 4096
FF = 16384
LEN = 64
PLANES = 4
CORES = 2
STEP = 1024
PIECES = 4


def chunk_kernel(k, rows, columns, *refs):
    own, other = refs[:columns], refs[columns : 2 * columns]
    mix, key_left, key_right, value_left, value_right, key, value = refs[2 * columns : 2 * columns + 7]
    keep, send, whole, natural, relative, natural_dots, dots = refs[2 * columns + 7 :]
    me = lax.axis_index("shard")
    core, y, plane = me % CORES, me // CORES % columns, me // (CORES * columns) ^ k
    tokens = rows * columns * CORES
    members = tokens // LEN

    def place(j, c):
        return pl.multiple_of(((y ^ j) * CORES + c) * rows, rows)

    def pick(array, member):
        at = lax.broadcasted_iota(jnp.int32, array.shape, 0) == member
        return jnp.sum(jnp.where(at, array.astype(jnp.float32), 0.0), 0, keepdims=True)

    for j in range(columns):
        whole[pl.ds(place(j, core), rows), :] = own[j][...]
        whole[pl.ds(place(j, 1 - core), rows), :] = other[j][...]

    inside = lax.broadcasted_iota(jnp.int32, (tokens, 1), 0) % LEN != 0
    total, along = None, [0.0] * members
    for start in range(0, D, STEP):
        at = slice(start, start + STEP)
        current = whole[:, at].astype(jnp.float32)
        previous = jnp.where(inside, pltpu.roll(current, 1, 0), 0.0)
        shifted = (current + (previous - current) * mix[:, at].astype(jnp.float32)).astype(jnp.bfloat16)
        part = jnp.dot(shifted, key[at, :], preferred_element_type=jnp.float32)
        total = part if total is None else total + part
        for m in range(members):
            wide = shifted[m * LEN : (m + 1) * LEN].astype(jnp.float32)
            products = wide * pick(key_left[:, at], plane * members + m)
            along[m] = along[m] + sum(products[:, i : i + 128] for i in range(0, STEP, 128))

    for m in range(members):
        at = slice(m * LEN, (m + 1) * LEN)
        dot = 0.5 / math.sqrt(D) * jnp.sum(along[m], 1, keepdims=True)
        hidden = total[at] + dot * pick(key_right[...], plane * members + m)
        keyed = jnp.square(jnp.maximum(hidden, 0.0)).astype(jnp.bfloat16)
        natural[at, :] = keyed
        dot = jnp.sum(keyed.astype(jnp.float32) * pick(value_left[...], plane * members + m), 1, keepdims=True)
        natural_dots[at, :] = jnp.broadcast_to(0.5 / math.sqrt(FF) * dot, (LEN, 128))

    cores = (core, 1 - core)
    for c in range(CORES):
        for j in range(columns):
            to = slice((c * columns + j) * rows, (c * columns + j + 1) * rows)
            relative[to, :] = natural[pl.ds(place(j, cores[c]), rows), :]
            dots[to, :] = natural_dots[pl.ds(place(j, cores[c]), rows), :]

    for start in range(0, D, STEP):
        at = slice(start, start + STEP)
        result = jnp.dot(relative[...], value[:, at], preferred_element_type=jnp.float32)
        for c, out in enumerate((keep, send)):
            for j in range(columns):
                to = slice((c * columns + j) * rows, (c * columns + j + 1) * rows)
                right = pick(value_right[:, at], plane * members + place(j, cores[c]) // LEN)
                out[j * rows : (j + 1) * rows, at] = (result[to] + dots[to, :1] * right).astype(jnp.bfloat16)


def chunk(k, own, other, mix, key_left, key_right, value_left, value_right, key, value):
    columns, rows = len(own), own[0].shape[0]
    hidden = key.shape[1]
    tokens = rows * columns * CORES
    operands = (*own, *other, mix, key_left, key_right, value_left, value_right, key, value)
    return pl.pallas_call(
        functools.partial(chunk_kernel, k, rows, columns),
        out_shape=[jax.ShapeDtypeStruct((columns * rows, D), jnp.bfloat16)] * 2,
        in_specs=[pl.BlockSpec(memory_space=pltpu.VMEM)] * len(operands),
        out_specs=[pl.BlockSpec(memory_space=pltpu.VMEM)] * 2,
        scratch_shapes=[
            pltpu.VMEM((tokens, D), jnp.bfloat16),
            pltpu.VMEM((tokens, hidden), jnp.bfloat16),
            pltpu.VMEM((tokens, hidden), jnp.bfloat16),
            pltpu.VMEM((tokens, 128), jnp.float32),
            pltpu.VMEM((tokens, 128), jnp.float32),
        ],
        compiler_params=pltpu.CompilerParams(vmem_limit_bytes=8 * 1024 * 1024),
        cost_estimate=pl.CostEstimate(flops=tokens, bytes_accessed=tokens, transcendentals=0),
    )(*operands)


def sum_kernel(rows, count, keep, arrived, *outs):
    both = keep[...].astype(jnp.float32) + arrived[...].astype(jnp.float32)
    at = 0
    for out in outs[:count]:
        out[...] = both[:rows, at : at + out.shape[1]].astype(out.dtype)
        at += out.shape[1]
    for j, out in enumerate(outs[count:], 1):
        out[...] = both[j * rows : (j + 1) * rows].astype(out.dtype)


def sum_cores(keep, arrived, columns, kind, widths=(D,)):
    rows = keep.shape[0] // columns
    outs = [jax.ShapeDtypeStruct((rows, width), kind) for width in widths]
    outs += [jax.ShapeDtypeStruct((rows, D), jnp.bfloat16)] * (columns - 1)
    return pl.pallas_call(
        functools.partial(sum_kernel, rows, len(widths)),
        out_shape=outs,
        in_specs=[pl.BlockSpec(memory_space=pltpu.VMEM)] * 2,
        out_specs=[pl.BlockSpec(memory_space=pltpu.VMEM)] * len(outs),
        compiler_params=pltpu.CompilerParams(vmem_limit_bytes=8 * 1024 * 1024),
        cost_estimate=pl.CostEstimate(flops=rows, bytes_accessed=rows, transcendentals=0),
    )(keep, arrived)


def pack_kernel(ranks, *refs):
    parts, out = refs[:-1], refs[-1]
    at = 0
    for part in parts:
        out[:, at : at + part.shape[1]] = part[...]
        at += part.shape[1]
    row = lax.broadcasted_iota(jnp.int32, (ranks.shape[0], 128), 0)
    marks = sum(jnp.where(row == m, ranks[m], 0) for m in range(ranks.shape[0]))
    out[:, at:] = marks.astype(jnp.float32).astype(jnp.bfloat16)


def pack_members(key_left, key_right, value_left, value_right, ranks):
    parts = (key_left, value_right, key_right, value_left)
    wide = sum(part.shape[1] for part in parts) + 128
    return pl.pallas_call(
        pack_kernel,
        out_shape=jax.ShapeDtypeStruct((ranks.shape[0], wide), jnp.bfloat16),
        in_specs=[pl.BlockSpec(memory_space=pltpu.SMEM)] + [pl.BlockSpec(memory_space=pltpu.VMEM)] * 4,
        out_specs=pl.BlockSpec(memory_space=pltpu.VMEM),
        compiler_params=pltpu.CompilerParams(vmem_limit_bytes=4 * 1024 * 1024),
        cost_estimate=pl.CostEstimate(flops=wide, bytes_accessed=wide, transcendentals=0),
    )(ranks, *parts)


def load_kernel(*refs):
    count = len(refs) // 2
    sems = refs[-1]
    copies = [pltpu.make_async_copy(refs[i], refs[count + i], sems.at[i]) for i in range(count)]
    for copy in copies:
        copy.start()
    for copy in copies:
        copy.wait()


def load(*arrays):
    size = sum(array.size * array.dtype.itemsize for array in arrays)
    return pl.pallas_call(
        load_kernel,
        out_shape=[jax.ShapeDtypeStruct(array.shape, array.dtype) for array in arrays],
        in_specs=[pl.BlockSpec(memory_space=pltpu.HBM)] * len(arrays),
        out_specs=[pl.BlockSpec(memory_space=pltpu.VMEM)] * len(arrays),
        scratch_shapes=[pltpu.SemaphoreType.DMA((len(arrays),))],
        compiler_params=pltpu.CompilerParams(vmem_limit_bytes=1024 * 1024),
        cost_estimate=pl.CostEstimate(flops=size // D, bytes_accessed=size // D, transcendentals=0),
    )(*arrays)


def update_kernel(fit_rows, piece, groups, hidden, count, *refs):
    packs, out, right = refs[:count], refs[-2], refs[-1]
    part, rows = D // groups, out.shape[0]

    def columns(start, size):
        at = pl.ds(pl.multiple_of(start, 128), size)
        return jnp.concatenate([ref[:, at].astype(jnp.float32) for ref in packs], 0)

    def split(array):
        everyone = array.shape[0]
        fitness = columns(packs[0].shape[1] - 128, 128)[:, :1] / (everyone - 1) - 0.5
        rest, terms = 2.0 / math.sqrt(everyone) * fitness * array, []
        for _ in range(3):
            terms.append(rest.astype(jnp.bfloat16).astype(jnp.float32))
            rest = rest - terms[-1]
        return jnp.concatenate(terms, 0).astype(jnp.bfloat16)

    def thrice(array):
        return jnp.concatenate([array] * 3, 0).astype(jnp.bfloat16)

    half = lax.axis_index("member") * part
    step = (piece * pl.num_programs(0) + pl.program_id(0)) * rows

    @pl.when(pl.program_id(0) == 0)
    def _():
        right[...] = thrice(columns(2 * D, hidden)) if fit_rows else split(columns(D + half, part))

    left = split(columns(half + step, rows)) if fit_rows else thrice(columns(2 * D + hidden + step, rows))
    out[...] = lax.dot_general(left, right[...], (((0,), (0,)), ((), ())), preferred_element_type=jnp.float32)


def update(fit_rows, packs, done, piece, groups, hidden):
    part = D // groups
    shape, rows = ((part, hidden), 256) if fit_rows else ((hidden, part), 128)
    rows = min(rows, shape[0] // PIECES)
    steps = shape[0] // rows // PIECES
    done = [] if done is None else [done]
    return pl.pallas_call(
        functools.partial(update_kernel, fit_rows, piece, groups, hidden, len(packs)),
        out_shape=jax.ShapeDtypeStruct(shape, jnp.float32),
        grid=(steps,),
        in_specs=[pl.BlockSpec(memory_space=pltpu.VMEM)] * len(packs) + [pl.BlockSpec(memory_space=pl.ANY)] * len(done),
        out_specs=pl.BlockSpec((rows, shape[1]), lambda i: (piece * steps + i, 0)),
        scratch_shapes=[pltpu.VMEM((3 * packs[0].shape[0] * len(packs), shape[1]), jnp.bfloat16)],
        input_output_aliases={len(packs): 0} if done else {},
        compiler_params=pltpu.CompilerParams(vmem_limit_bytes=12 * 1024 * 1024),
        cost_estimate=pl.CostEstimate(flops=rows, bytes_accessed=rows, transcendentals=0),
    )(*packs, *done)


def together(*values):
    return lax.optimization_barrier(values)


def local(
    tokens, key_weight, value_weight, shift_mix, key_left, key_right, value_left, value_right, ranks
):
    devices, groups = lax.axis_size("shard"), lax.axis_size("member")
    columns = devices // (PLANES * CORES)
    rows, hidden = tokens.shape[0], key_weight.shape[1]

    def swap(array, bits):
        return lax.ppermute(array, "shard", [(i, i ^ bits) for i in range(devices)])

    def over_z(array, k):
        return swap(array, k * columns * CORES)

    def over_y(array):
        return [swap(array, j * CORES) for j in range(1, columns)]

    def over_both(array):
        return [swap(array, (columns + j) * CORES) for j in range(1, columns)]

    def over_cores(arrays):
        return [swap(array, 1) for array in arrays]

    def back_y(terms):
        return [swap(term, j * CORES) for j, term in enumerate(terms, 1)]

    def updates(fit_rows, packs, done, start, stop):
        for piece in range(start, stop):
            done = update(fit_rows, packs, done, piece, groups, hidden)
        return done

    def add(mine, arrived):
        return functools.reduce(lambda total, part: total + part.astype(jnp.float32), arrived, mine)

    def by_block(*blocks):
        return [list(block) for block in zip(*blocks)]

    def rounded(array):
        return array.astype(jnp.bfloat16)

    far, near, y0, c0 = over_z(tokens, 2), over_z(tokens, 1), over_y(tokens), over_cores([tokens])
    near, y0, c0, mix, key = together(near, y0, c0, shift_mix[None, :], key_weight)

    y1, cy0, c1 = over_y(near), over_cores(y0), over_cores([near])
    (key,) = load(key)
    far, y1, cy0, c1, key, value, left = together(far, y1, cy0, c1, key, value_weight, key_left)

    (value,) = load(value)
    pack = pack_members(left, key_right, value_left, value_right, ranks)
    packs = [pack] + [
        lax.ppermute(pack, "member", [(i, i ^ bits) for i in range(groups)]) for bits in range(1, groups)
    ]

    def partial(k, own, other):
        return chunk(k, own, other, mix, key_left, key_right, value_left, value_right, key, value)

    farthest, y2, y3, c2, cy1 = over_z(far, 1), over_y(far), over_both(far), over_cores([far]), over_cores(y1)
    keep1, send1 = partial(1, [near] + y1, c1 + cy1)
    own, keep1 = together(tokens, keep1)
    keep0, send0 = partial(0, [own] + y0, c0 + cy0)
    packs, keep0 = together(packs, keep0)
    key_update = updates(True, packs, None, 0, 1)
    farthest, y2, y3, c2, keep1, send1, send0, key_update = together(
        farthest, y2, y3, c2, keep1, send1, send0, key_update
    )

    c3, cy3, cy2, other1 = over_cores([farthest]), over_cores(y3), over_cores(y2), over_cores([send1])
    keep3, send3 = partial(3, [farthest] + y3, c3 + cy3)
    cy2, other1, keep3, send3 = together(cy2, other1, keep3, send3)

    first1, second1, mine1, *terms1 = sum_cores(
        keep1, *other1, columns, jnp.bfloat16, (D // 4, D // 4, D // 2)
    )
    beside1, first1 = [over_z(term, 1) for term in terms1], over_z(first1, 1)
    mine3, *terms3 = sum_cores(keep3, *over_cores([send3]), columns, jnp.float32)
    far, mine3, terms3 = together(far, mine3, terms3)
    back3 = back_y(terms3)
    keep2, send2 = partial(2, [far] + y2, c2 + cy2)
    packs, keep2 = together(packs, keep2)
    key_update = updates(True, packs, key_update, 1, 2)
    beside1, back3, keep2, send2, send0, packs, mine1, key_update, first1, second1 = together(
        beside1, back3, keep2, send2, send0, packs, mine1, key_update, first1, second1
    )

    onward, early = over_z(rounded(add(mine3, back3)), 1), over_z(second1, 1)
    other0, other2 = over_cores([send0, send2])
    mine2, *terms2 = sum_cores(keep2, other2, columns, jnp.float32)
    packs, mine2, terms2 = together(packs, mine2, terms2)
    back2 = back_y(terms2)
    key_update = updates(True, packs, key_update, 2, 4)
    onward, mine2, back2, other0, key_update, packs, mine1, early = together(
        onward, mine2, back2, other0, key_update, packs, mine1, early
    )

    last = over_z(rounded(add(mine2, back2 + [onward])), 2)
    both = keep0.astype(jnp.float32) + other0.astype(jnp.float32)
    terms0 = [rounded(add(both[j * rows : (j + 1) * rows], [term])) for j, term in enumerate(beside1, 1)]
    back0, mine1 = back_y(terms0), jnp.concatenate([first1, early, over_z(mine1, 1)], 1)
    value_update = updates(False, packs, None, 0, 4)
    return rounded(add(both[:rows], [last, mine1] + back0)), key_update, value_update


def solution(mesh):
    placed = (
        P(("member", "shard"), None),
        P(None, "shard"),
        P("shard", None),
        P(),
        P("member", None),
        P("member", "shard"),
        P("member", "shard"),
        P("member", None),
        P("member"),
    )
    return jax.shard_map(
        local,
        mesh=mesh,
        in_specs=placed,
        out_specs=(P(("member", "shard"), None), P("member", "shard"), P("shard", "member")),
        check_vma=False,
    )
```
